128 devices in a mesh: img: 8 (over z, core), txt: 16 (over y, x).
Axes of the slice: x: 4, y: 4, z: 4, core: 2. Of those that a mesh axis runs over, the one named last changes fastest.
Arguments:
- image_emb: bfloat16 [196608, 1152], P(('img', 'txt')), may hold values from -0.1796875 to 0.1796875
- text_emb: bfloat16 [196608, 1152], P(('img', 'txt')), may hold values from -0.1796875 to 0.1796875
- row_weight: bfloat16 [196608], P(('img', 'txt')), may hold values from 0.5 to 6
- log_scale: float32 [1], replicated, may hold values from 1.6 to 2.4
- bias: float32 [1], replicated, may hold values from -4 to -2
- pair_slots: int32 [2048, 3], P(('img', 'txt')), may hold values from 0 to 3, as said below
Outputs:
- grad_image: bfloat16 [196608, 1152], P(('img', 'txt'))
- grad_text: bfloat16 [196608, 1152], P(('img', 'txt'))
- totals: float32 [3], replicated
The draws below stay inside these ranges and needn't reach their ends.
Inputs may be any that keep to these rules, and one draw needn't show every extreme that they name: `pair_slots`: entries 0 and 1 are block numbers below 4; entry 2 is 0 or 1; a device's row at its own txt index has live 0; no device has more than 12 live rows, and in every draw some device has exactly 12.
All inputs are finite; a program needn't handle non-finite values.
Results may differ from the reference program's by a relative error of at most 0.009.
Values may be sent and summed in bfloat16 or wider, within the bound.
No kernel may reach another device: no remote copies, remote signals or barrier semaphores. Data moves between devices by JAX's collectives and lax.ppermute only.
A program may use at most 192 MiB of HBM per device.

```python
import jax
import jax.numpy as jnp
from jax import lax

D = 1152
ROWS = 384
BLK = 4
ROWS_ALL = 196608
LIVE_MOST = 12
N_IMG = 8
N_TXT = 16


def draw_row_weight(key, part):
    key = jax.random.fold_in(key, 12)
    total = BLK * ROWS * N_IMG * N_TXT
    ramp = 1.0 + 2.0 * jnp.arange(total, dtype=jnp.float32) / (total - 1)
    base = jnp.exp(jax.random.uniform(key, (total,), jnp.float32, jnp.log(0.5), jnp.log(2.0)))
    return (base * ramp).astype(jnp.bfloat16)


def draw_pair_slots(key, part):
    key = jax.random.fold_in(key, 11)
    keys = jax.random.split(key, 5)
    ndev = N_IMG * N_TXT
    image_idx = jax.random.randint(keys[0], (ndev, N_TXT), 0, BLK)
    text_idx = jax.random.randint(keys[1], (ndev, N_TXT), 0, BLK)
    rate = jax.random.randint(keys[2], (ndev, 1), 2, 10)
    roll = jax.random.randint(keys[3], (ndev, N_TXT), 0, 10)
    busiest = jax.random.randint(keys[4], (), 0, ndev)
    device = jnp.arange(ndev, dtype=jnp.int32)[:, None]
    peer = jnp.arange(N_TXT, dtype=jnp.int32)[None, :]
    wanted = (roll < rate) | (device == busiest)
    wanted = wanted & (device % N_TXT != peer)
    rank = jnp.cumsum(wanted.astype(jnp.int32), axis=1)
    live = wanted & (rank <= LIVE_MOST)
    table = jnp.stack([image_idx, text_idx, live.astype(jnp.int32)], axis=-1)
    return table.reshape(ndev * N_TXT, 3).astype(jnp.int32)


def levels(own_key, extent, pieces, low, largest):
    def one(dim, blocks):
        draws = jax.random.uniform(jax.random.fold_in(jax.random.fold_in(own_key, 6), dim), (blocks,), jnp.float32, low / len(pieces), largest / len(pieces))
        return jnp.repeat(jnp.exp(draws), extent[dim] // blocks).reshape((-1,) + (1,) * (len(extent) - dim - 1))

    factor_of = one(*pieces[0])
    for cut in pieces[1:]:
        factor_of = factor_of * one(*cut)
    return factor_of


def noise(own_key, extent, width, most, pieces=(), kind=jnp.bfloat16):
    result = jax.random.normal(own_key, extent, jnp.float32) * width
    if len(pieces) > 0:
        result = levels(own_key, extent, pieces, -0.22, 0.18) * result
    return jnp.clip(result, min=-most, max=most).astype(kind)


def setup_inputs(seed: int = 0) -> dict:
    arg_keys = jax.random.split(jax.random.key(seed), 7)
    image_emb = noise(arg_keys[0], (ROWS_ALL, D), 0.03, 0.1796875, ((0, 128),))
    text_emb = noise(arg_keys[1], (ROWS_ALL, D), 0.03, 0.1796875, ((0, 128),))
    row_weight = draw_row_weight(jax.random.fold_in(arg_keys[6], 71), 0)
    log_scale = jnp.clip(jax.random.uniform(arg_keys[3], (1,), jnp.float32, 1.6, 2.4), 1.6, 2.4)
    bias = jnp.clip(jax.random.uniform(arg_keys[4], (1,), jnp.float32, -4.0, -2.0), -4.0, -2.0)
    pair_slots = draw_pair_slots(jax.random.fold_in(arg_keys[6], 71), 0)
    return dict(image_emb=image_emb, text_emb=text_emb, row_weight=row_weight, log_scale=log_scale, bias=bias, pair_slots=pair_slots)


EPS = 1e-06

def normalize(emb):
    values = emb.astype(jnp.float32)
    inverse = lax.rsqrt(lax.optimization_barrier(jnp.sum(values * values, axis=-1, keepdims=True)) + EPS)
    return (values * inverse).astype(jnp.bfloat16)

def pair_tiles(image_blk, text_blk, weights, scale, offset, positive):
    sims = jnp.dot(image_blk, text_blk.T, preferred_element_type=jnp.float32)
    logits = scale * sims + offset
    eye = jnp.eye(image_blk.shape[0], dtype=jnp.float32)
    signs = 2.0 * positive * eye - 1.0
    wcol = weights[:, None]
    loss = -wcol * jax.nn.log_sigmoid(signs * logits)
    grads = -wcol * signs * jax.nn.sigmoid(-signs * logits)
    scaled = (scale * grads).astype(jnp.bfloat16)
    d_image = jnp.dot(scaled, text_blk, preferred_element_type=jnp.float32)
    d_text = jnp.dot(scaled.T, image_blk, preferred_element_type=jnp.float32)
    stats = jnp.stack([jnp.sum(loss), jnp.sum(grads * scale * sims), jnp.sum(grads)])
    return (d_image, d_text, stats)

def backprop_norm(emb, grad_hat):
    values = emb.astype(jnp.float32)
    inverse = lax.rsqrt(lax.optimization_barrier(jnp.sum(values * values, axis=-1, keepdims=True)) + EPS)
    unit = values * inverse
    inner = lax.optimization_barrier(jnp.sum(unit * grad_hat, axis=-1, keepdims=True))
    return (inverse * (grad_hat - unit * inner)).astype(jnp.bfloat16)

def reference(image_emb, text_emb, row_weight, log_scale, bias, pair_slots):
    ndev = N_IMG * N_TXT
    scale = jnp.exp(log_scale[0])
    offset = bias[0]
    image_hat = normalize(image_emb).reshape(ndev, BLK, ROWS, D)
    text_hat = normalize(text_emb).reshape(ndev, BLK, ROWS, D)
    weights_all = row_weight.astype(jnp.float32).reshape(ndev, BLK, ROWS)
    slots = pair_slots.reshape(ndev, N_TXT, 3)

    def per_device(carry, device):
        text_grads, stats = carry
        own_images = image_hat[device]
        own_texts = text_hat[device]
        own_weights = weights_all[device]
        image_tiles = []
        for block in range(BLK):
            d_image, d_text, part = pair_tiles(own_images[block], own_texts[block], own_weights[block], scale, offset, 1.0)
            image_tiles.append(d_image)
            text_grads = text_grads.at[device, block].add(d_text)
            stats = stats + part
        image_acc = jnp.stack(image_tiles)

        def per_slot(inner, slot):
            image_acc, text_grads, stats = inner
            entry = slots[device, slot]
            peer = device // N_TXT * N_TXT + slot
            live = entry[2].astype(jnp.float32)
            text_blk = text_hat[peer, entry[1]]
            d_image, d_text, part = pair_tiles(own_images[entry[0]], text_blk, own_weights[entry[0]] * live, scale, offset, 0.0)
            image_acc = image_acc.at[entry[0]].add(d_image.astype(jnp.bfloat16).astype(jnp.float32))
            text_grads = text_grads.at[peer, entry[1]].add(d_text.astype(jnp.bfloat16).astype(jnp.float32))
            return ((image_acc, text_grads, stats + part), None)
        (image_acc, text_grads, stats), _ = lax.scan(per_slot, (image_acc, text_grads, stats), jnp.arange(N_TXT, dtype=jnp.int32))
        return ((text_grads, stats), image_acc)
    start = (jnp.zeros((ndev, BLK, ROWS, D), jnp.float32), jnp.zeros((3,), jnp.float32))
    (text_grads, stats), image_grads = lax.scan(per_device, start, jnp.arange(ndev, dtype=jnp.int32))
    grad_image = backprop_norm(image_emb, image_grads.reshape(ROWS_ALL, D))
    grad_text = backprop_norm(text_emb, text_grads.reshape(ROWS_ALL, D))
    return (grad_image, grad_text, stats / ROWS_ALL)
```

```python
import functools

import jax
import jax.numpy as jnp
from jax import lax
from jax.experimental import pallas as pl
from jax.experimental.pallas import tpu as pltpu
from jax.sharding import PartitionSpec as P

ROWS = 384
BLK = 4
SIDE = 4
HALF = BLK // 2
EPS = 1e-06
VMEM = 60 * 1024 * 1024
CHUNK = 48

NEAR = (0, 1, 3)
FAR = 2
NEAR_SLOTS = tuple((i, j) for i in NEAR for j in NEAR if (i, j) != (0, 0))
FAR_X_SLOTS = tuple((FAR, j) for j in (0, 1, 3, 2))
FAR_Y_SLOTS = tuple((i, FAR) for i in NEAR)
ALL_SLOTS = NEAR_SLOTS + FAR_X_SLOTS + FAR_Y_SLOTS
SLOT_AT = {slot: at for at, slot in enumerate(ALL_SLOTS)}
N_SLOTS = len(ALL_SLOTS)
ANY = pl.BlockSpec(memory_space=pl.ANY)
SMEM = pl.BlockSpec(memory_space=pltpu.SMEM)
WHOLE = pl.BlockSpec(memory_space=pltpu.VMEM)


def params(flops, nbytes):
    return dict(
        compiler_params=pltpu.CompilerParams(vmem_limit_bytes=VMEM),
        cost_estimate=pl.CostEstimate(flops=flops, bytes_accessed=nbytes, transcendentals=0),
    )


def normalize_kernel(emb_ref, out_ref):
    values = emb_ref[...].astype(jnp.float32)
    inverse = lax.rsqrt(jnp.sum(values * values, axis=-1, keepdims=True) + EPS)
    out_ref[...] = (values * inverse).astype(jnp.bfloat16)


def normalize(emb):
    rows, width = emb.shape
    spec = pl.BlockSpec((ROWS, width), lambda g: (g, 0))
    return pl.pallas_call(
        normalize_kernel,
        grid=(rows // ROWS,),
        in_specs=[spec],
        out_specs=spec,
        out_shape=jax.ShapeDtypeStruct(emb.shape, jnp.bfloat16),
        **params(rows * width * 6, rows * width * 4),
    )(emb)


def block_copies(refs, offset, index, dst, sem):
    found = refs[offset]
    if len(found) == 1:
        rows = pl.ds(pl.multiple_of(index * ROWS, ROWS), ROWS)
        return [(None, pltpu.make_async_copy(found[0].at[rows], dst, sem))]
    copies = []
    for part in range(2):
        local = jnp.clip(index - part * HALF, 0, HALF - 1)
        rows = pl.ds(pl.multiple_of(local * ROWS, ROWS), ROWS)
        inside = (index >= part * HALF) & (index < (part + 1) * HALF)
        copies.append((inside, pltpu.make_async_copy(found[part].at[rows], dst, sem)))
    return copies


def start_copies(live, copies):
    for inside, copy in copies:
        go = live if inside is None else live & inside
        pl.when(go)(copy.start)


def split_refs(refs):
    return {0: refs[0:1], 1: refs[1:2], 2: refs[2:4], 3: refs[4:5]}


def coefficients(sims_ref, coef_ref, weight_ref, scale, offset, positive):
    def step(at, sums):
        loss_sum, coef_sum, dot_sum = sums
        rows = pl.ds(pl.multiple_of(at * CHUNK, CHUNK), CHUNK)
        sims = sims_ref[rows, :]
        logits = scale * sims + offset
        weight = jnp.concatenate([weight_ref[rows, :]] * (ROWS // 128), axis=1)
        scaled_weight = weight * scale
        if positive is not None:
            row = lax.broadcasted_iota(jnp.int32, sims.shape, 0) + at * CHUNK
            col = lax.broadcasted_iota(jnp.int32, sims.shape, 1)
            diagonal = (row == col) & (positive > 0)
            logits = jnp.where(diagonal, -logits, logits)
            scaled_weight = jnp.where(diagonal, -scaled_weight, scaled_weight)
        power = jnp.exp(logits)
        one_more = 1.0 + power
        coef = scaled_weight * (power / one_more)
        loss = weight * jnp.log(one_more)
        coef_ref[rows, :] = coef.astype(jnp.bfloat16)

        def fold(value):
            return jnp.sum(value.reshape(CHUNK // 8, 8, ROWS), axis=0)

        return (loss_sum + fold(loss), coef_sum + fold(coef), dot_sum + fold(coef * sims))

    zero = jnp.zeros((8, ROWS), jnp.float32)
    return lax.fori_loop(0, ROWS // CHUNK, step, (zero, zero, zero))


def dot(lhs, rhs, dims):
    return lax.dot_general(lhs, rhs, (dims, ((), ())), preferred_element_type=jnp.float32)


NT = ((1,), (1,))
NN = ((1,), (0,))
TN = ((0,), (0,))


def pairs_kernel(slots, n_positive, out_axis, n_extra, *refs):
    meta, scalars, weights = refs[0:3]
    xrefs, yrefs = split_refs(refs[3:8]), split_refs(refs[8:13])
    at = 13
    extra_coef = refs[at] if n_extra else None
    at += 1 if n_extra else 0
    coef_out, stats_out = refs[at], refs[at + 1]
    at += 2
    grads = refs[at:at + 2] if out_axis else ()
    at += len(grads)
    xbuf, ybuf, wbuf, sims, sems = refs[at:at + 5]
    acc = refs[at + 5] if out_axis else None
    total = len(slots) + n_positive
    scale, offset = scalars[0], scalars[1]

    def entry(s):
        if s < len(slots):
            base = SLOT_AT[slots[s]]
            return base, slots[s]
        return N_SLOTS + s - len(slots), (0, 0)

    for s in range(total):
        row, (i, j) = entry(s)
        live = meta[row, 2] > 0
        p, q = meta[row, 0], meta[row, 1]
        start_copies(live, block_copies(xrefs, i, p, xbuf.at[s], sems.at[0, s]))
        start_copies(live, block_copies(yrefs, j, q, ybuf.at[s], sems.at[1, s]))
        rows = pl.ds(pl.multiple_of((i * BLK + p) * ROWS, ROWS), ROWS)
        start_copies(live, [(None, pltpu.make_async_copy(weights.at[rows], wbuf.at[s], sems.at[2, s]))])
    extra = ()
    if n_extra:
        row = SLOT_AT[(FAR, FAR)]
        live_extra = meta[row, 2] > 0
        extra = [(xbuf.at[total], sems.at[0, total]), (ybuf.at[total, :, :ROWS], sems.at[1, total])]
        start_copies(live_extra, block_copies(xrefs, FAR, meta[row, 0], *extra[0]))
        coef_copy = pltpu.make_async_copy(extra_coef.at[FAR_X_SLOTS.index((FAR, FAR))], *extra[1])
        start_copies(live_extra, [(None, coef_copy)])

    stats_out[...] = jnp.zeros_like(stats_out)
    if out_axis:
        for b in range(BLK):
            acc[b] = jnp.zeros_like(acc[b])

    first = SLOT_AT[slots[0]]

    def work(s, unused):
        row = jnp.where(s < len(slots), first + s, N_SLOTS + s - len(slots))

        @pl.when(meta[row, 2] > 0)
        def _():
            pltpu.make_async_copy(xrefs[0][0].at[pl.ds(0, ROWS)], xbuf.at[s], sems.at[0, s]).wait()
            pltpu.make_async_copy(yrefs[0][0].at[pl.ds(0, ROWS)], ybuf.at[s], sems.at[1, s]).wait()
            pltpu.make_async_copy(weights.at[pl.ds(0, ROWS)], wbuf.at[s], sems.at[2, s]).wait()
            sims[...] = dot(xbuf[s], ybuf[s], NT)
            positive = meta[row, 3] if n_positive else None
            sums = coefficients(sims, coef_out.at[s], wbuf.at[s], scale, offset, positive)
            for k in range(3):
                stats_out[k] += sums[k]
            if out_axis == "x":
                acc[meta[row, 0]] += dot(coef_out[s], ybuf[s], NN)
            if out_axis == "y":
                acc[meta[row, 1]] += dot(coef_out[s], xbuf[s], TN)

        return unused

    lax.fori_loop(0, total, work, 0)
    if n_extra:
        @pl.when(live_extra)
        def _():
            pltpu.make_async_copy(xrefs[0][0].at[pl.ds(0, ROWS)], *extra[0]).wait()
            pltpu.make_async_copy(extra_coef.at[0], *extra[1]).wait()
            acc[meta[SLOT_AT[(FAR, FAR)], 1]] += dot(ybuf[total, :, :ROWS], xbuf[total], TN)
    for b in range(BLK if out_axis else 0):
        grads[b // HALF][pl.ds(b % HALF * ROWS, ROWS), :] = acc[b].astype(jnp.bfloat16)


def pairs(slots, n_positive, out_axis, extra_coef, meta, scalars, weights, images, texts):
    width = images[0].shape[1]
    total = len(slots) + n_positive
    n_extra = 0 if extra_coef is None else 1
    out_shape = [
        jax.ShapeDtypeStruct((total, ROWS, ROWS), jnp.bfloat16),
        jax.ShapeDtypeStruct((3, 8, ROWS), jnp.float32),
    ]
    if out_axis:
        out_shape += [jax.ShapeDtypeStruct((HALF * ROWS, width), jnp.bfloat16)] * 2
    held = total + n_extra
    scratch = [
        pltpu.VMEM((held, ROWS, width), jnp.bfloat16),
        pltpu.VMEM((held, ROWS, width), jnp.bfloat16),
        pltpu.VMEM((total, ROWS, 128), jnp.float32),
        pltpu.VMEM((ROWS, ROWS), jnp.float32),
        pltpu.SemaphoreType.DMA((3, held)),
    ]
    if out_axis:
        scratch.append(pltpu.VMEM((BLK, ROWS, width), jnp.float32))
    operands = [meta, scalars, weights, *images, *texts]
    specs = [SMEM, SMEM] + [ANY] * 11
    if n_extra:
        operands.append(extra_coef)
        specs.append(ANY)
    matmuls = total + (held if out_axis else 0)
    return pl.pallas_call(
        functools.partial(pairs_kernel, slots, n_positive, out_axis, n_extra),
        in_specs=specs,
        out_specs=[WHOLE] * len(out_shape),
        out_shape=out_shape,
        scratch_shapes=scratch,
        **params(matmuls * 2 * ROWS * ROWS * width * 2, total * 2 * ROWS * width * 2),
    )(*operands)


def grads_kernel(axis, groups, sources, *refs):
    meta = refs[0]
    other = split_refs(refs[1:6])
    coefs = refs[6:6 + sources]
    outs = refs[6 + sources:6 + sources + len(groups)]
    buf, cbuf, acc, sems = refs[6 + sources + len(groups):]
    mine, theirs = (0, 1) if axis == "x" else (1, 0)
    at = 0
    for group in groups:
        for row, source, index, neighbour in group:
            live = meta[row, 2] > 0
            start_copies(live, block_copies(other, neighbour, meta[row, theirs], buf.at[at], sems.at[0, at]))
            copy = pltpu.make_async_copy(coefs[source].at[index], cbuf.at[at], sems.at[1, at])
            start_copies(live, [(None, copy)])
            at += 1
    at = 0
    for group, out in zip(groups, outs):
        for b in range(BLK):
            acc[b] = jnp.zeros_like(acc[b])
        for row, source, index, neighbour in group:

            @pl.when(meta[row, 2] > 0)
            def _():
                pltpu.make_async_copy(other[0][0].at[pl.ds(0, ROWS)], buf.at[at], sems.at[0, at]).wait()
                pltpu.make_async_copy(coefs[source].at[index], cbuf.at[at], sems.at[1, at]).wait()
                acc[meta[row, mine]] += dot(cbuf[at], buf[at], NN if axis == "x" else TN)

            at += 1
        for b in range(BLK):
            out[pl.ds(b * ROWS, ROWS), :] = acc[b].astype(out.dtype)


def grads(axis, offsets, with_positive, dtype, meta, blocks, near, far_x, far_y):
    width = blocks[0].shape[1]
    groups = []
    for offset in offsets:
        group = []
        for neighbour in (0, 1, 3, 2):
            slot = (offset, neighbour) if axis == "x" else (neighbour, offset)
            if slot == (0, 0):
                continue
            for source, known in enumerate((NEAR_SLOTS, FAR_X_SLOTS, FAR_Y_SLOTS)):
                if slot in known:
                    group.append((SLOT_AT[slot], source, known.index(slot), neighbour))
        if with_positive:
            for b in range(BLK):
                group.append((N_SLOTS + b, 0, len(NEAR_SLOTS) + b, 0))
        groups.append(tuple(group))
    total = sum(len(group) for group in groups)
    return pl.pallas_call(
        functools.partial(grads_kernel, axis, tuple(groups), 3),
        in_specs=[SMEM] + [ANY] * 8,
        out_specs=[WHOLE] * len(groups),
        out_shape=[jax.ShapeDtypeStruct((BLK * ROWS, width), dtype)] * len(groups),
        scratch_shapes=[
            pltpu.VMEM((total, ROWS, width), jnp.bfloat16),
            pltpu.VMEM((total, ROWS, ROWS), jnp.bfloat16),
            pltpu.VMEM((BLK, ROWS, width), jnp.float32),
            pltpu.SemaphoreType.DMA((2, total)),
        ],
        **params(total * 2 * ROWS * ROWS * width * 2, total * 2 * ROWS * width * 2),
    )(meta, *blocks, near, far_x, far_y)


def finish_kernel(emb_ref, own_ref, left_ref, right_ref, out_ref):
    values = emb_ref[...].astype(jnp.float32)
    inverse = lax.rsqrt(jnp.sum(values * values, axis=-1, keepdims=True) + EPS)
    unit = values * inverse
    total = own_ref[...] + left_ref[...].astype(jnp.float32) + right_ref[...].astype(jnp.float32)
    inner = jnp.sum(unit * total, axis=-1, keepdims=True)
    out_ref[...] = (inverse * (total - unit * inner)).astype(jnp.bfloat16)


def finish(emb, own, left, right):
    rows, width = emb.shape
    step = 256
    spec = pl.BlockSpec((step, width), lambda g: (g, 0))
    return pl.pallas_call(
        finish_kernel,
        grid=(rows // step,),
        in_specs=[spec] * 4,
        out_specs=spec,
        out_shape=jax.ShapeDtypeStruct(emb.shape, jnp.bfloat16),
        **params(rows * width * 12, rows * width * 12),
    )(emb, own, left, right)


def shift(value, axis, by):
    pairs_of = []
    for y in range(SIDE):
        for x in range(SIDE):
            to = (y * SIDE + (x + by) % SIDE) if axis == "x" else ((y + by) % SIDE * SIDE + x)
            pairs_of.append((y * SIDE + x, to))
    return lax.ppermute(value, "txt", pairs_of)


def after(values, done):
    out = lax.optimization_barrier(tuple(values) + tuple(done))
    return out[:len(values)]


def per_device(image_emb, text_emb, row_weight, log_scale, bias, pair_slots):
    half = HALF * ROWS
    scale = jnp.exp(log_scale[0])
    scalars = jnp.stack([scale, bias[0]])
    xh, yh = normalize(image_emb), normalize(text_emb)
    x_prev, x_next = shift(xh, "x", 1), shift(xh, "x", -1)
    y_prev, y_next = shift(yh, "y", 1), shift(yh, "y", -1)

    small = jnp.concatenate([row_weight.astype(jnp.float32), pair_slots.astype(jnp.float32).reshape(-1)])
    everyone = lax.all_gather(small, "txt", axis=0, tiled=False)
    me = lax.axis_index("txt")
    my_y, my_x = me // SIDE, me % SIDE
    row_devices = jnp.stack([my_y * SIDE + (my_x + i) % SIDE for i in range(SIDE)])
    row_data = jnp.take(everyone, row_devices, axis=0)
    weights = row_data[:, :BLK * ROWS].reshape(SIDE * BLK * ROWS, 1)
    weights = jnp.broadcast_to(weights, (SIDE * BLK * ROWS, 128))
    plans = row_data[:, BLK * ROWS:].reshape(SIDE, SIDE, SIDE, 3)
    plans = lax.dynamic_index_in_dim(plans, my_x, axis=2, keepdims=False)
    plans = jnp.roll(plans, -my_y, axis=1)
    table = [plans[i, j] for i, j in ALL_SLOTS]
    negative = jnp.concatenate([jnp.stack(table), jnp.zeros((N_SLOTS, 1), jnp.float32)], axis=1)
    numbers = jnp.arange(BLK, dtype=jnp.float32)
    positive = jnp.stack([numbers, numbers, jnp.ones(BLK), jnp.ones(BLK)], axis=1)
    meta = jnp.concatenate([negative, positive]).astype(jnp.int32)

    x_prev, x_next, y_prev, y_next = after((x_prev, x_next, y_prev, y_next), ())
    x_far = (shift(x_prev[:half], "x", 1), shift(x_next[half:], "x", -1))
    y_far = (shift(y_prev[:half], "y", 1), shift(y_next[half:], "y", -1))
    near_images = (xh, x_next, xh, xh, x_prev)
    near_texts = (yh, y_next, yh, yh, y_prev)
    near, near_stats = pairs(NEAR_SLOTS, BLK, None, None, meta, scalars, weights, near_images, near_texts)

    images = (xh, x_next, *x_far, x_prev)
    texts = (yh, y_next, *y_far, y_prev)
    far_x, far_x_stats, dx_a, dx_b = pairs(FAR_X_SLOTS, 0, "x", None, meta, scalars, weights, images, texts)
    dx_from_prev, dx_from_next = shift(dx_a, "x", 1), shift(dx_b, "x", -1)
    far_y, far_y_stats, dy_a, dy_b = pairs(FAR_Y_SLOTS, 0, "y", far_x, meta, scalars, weights, images, texts)
    dy_from_prev, dy_from_next = shift(dy_a, "y", 1), shift(dy_b, "y", -1)
    dx_next, dx_prev = grads("x", (1, 3), False, jnp.bfloat16, meta, texts, near, far_x, far_y)
    dy_next, dy_prev = grads("y", (1, 3), False, jnp.bfloat16, meta, images, near, far_x, far_y)

    def join(ours, arrived, lower):
        summed = (ours[:half] if lower else ours[half:]).astype(jnp.float32) + arrived.astype(jnp.float32)
        summed = summed.astype(jnp.bfloat16)
        return jnp.concatenate([summed, ours[half:]] if lower else [ours[:half], summed])

    back_x = (shift(join(dx_next, dx_from_prev, True), "x", 1), shift(join(dx_prev, dx_from_next, False), "x", -1))
    back_y = (shift(join(dy_next, dy_from_prev, True), "y", 1), shift(join(dy_prev, dy_from_next, False), "y", -1))
    (dx_own,) = grads("x", (0,), True, jnp.float32, meta, texts, near, far_x, far_y)
    (dy_own,) = grads("y", (0,), True, jnp.float32, meta, images, near, far_x, far_y)

    sums = jnp.sum((near_stats + far_x_stats + far_y_stats).reshape(3, -1), axis=1)
    stats = jnp.stack([sums[0], sums[2], sums[1] / scale])
    summed = lax.psum(stats, ("img", "txt"))
    count = BLK * ROWS * lax.axis_size("img") * lax.axis_size("txt")
    grad_image = finish(image_emb, dx_own, *back_x)
    grad_text = finish(text_emb, dy_own, *back_y)
    return (grad_image, grad_text, summed / count)


def solution(mesh):
    return jax.shard_map(
        per_device,
        mesh=mesh,
        in_specs=(
            P(("img", "txt"), None),
            P(("img", "txt"), None),
            P(("img", "txt")),
            P(),
            P(),
            P(("img", "txt"), None),
        ),
        out_specs=(P(("img", "txt"), None), P(("img", "txt"), None), P()),
        check_vma=False,
    )
```

```python
import functools

import jax
import jax.numpy as jnp
from jax import lax
from jax.experimental import pallas as pl
from jax.experimental.pallas import tpu as pltpu
from jax.sharding import PartitionSpec as P

ROWS = 384
BLK = 4
SIDE = 4
HALF = BLK // 2
EPS = 1e-06
VMEM = 60 * 1024 * 1024
CHUNK = 48

FAR = 2
EARLY = ((0, 1), (0, 3), (FAR, 0), (FAR, 1), (FAR, 3))
OPPOSITE = ((FAR, FAR), (0, FAR), (1, FAR), (3, FAR))
LATE = tuple((i, j) for i in (1, 3) for j in (0, 1, 3))
GROUPS = (EARLY, OPPOSITE, LATE)
COEF_AT = {slot: (source, known.index(slot)) for source, known in enumerate(GROUPS) for slot in known}
POSITIVE = "positive"
SLOT_NUMBERS = 3 * SIDE * SIDE
NOTES = 16
ANY = pl.BlockSpec(memory_space=pl.ANY)
SMEM = pl.BlockSpec(memory_space=pltpu.SMEM)
WHOLE = pl.BlockSpec(memory_space=pltpu.VMEM)


def params():
    return dict(
        compiler_params=pltpu.CompilerParams(vmem_limit_bytes=VMEM),
        cost_estimate=pl.CostEstimate(flops=1000, bytes_accessed=1000, transcendentals=0),
    )


def pipelined(items, ahead):
    for start, _, _ in items[:ahead]:
        start()
    for at, (_, wait, work) in enumerate(items):
        wait()
        if at + ahead < len(items):
            items[at + ahead][0]()
        work()


def chunked(chunks, sources, targets, work):
    def item(c):
        def start():
            for copy in sources[c]:
                copy.start()

        def wait():
            for copy in sources[c]:
                copy.wait()

        def run():
            work(c)
            targets[c].start()

        return start, wait, run

    pipelined([item(c) for c in range(chunks)], chunks)
    for copy in targets:
        copy.wait()


def normalize_kernel(chunks, images, texts, notes, xa, xb, ya, yb, held, done, sems, note_sems):
    half = images.shape[0] // 2
    step = 2 * half // chunks
    note_copies = [
        pltpu.make_async_copy(notes, out.at[pl.ds(half, NOTES)], note_sems.at[k]) for k, out in enumerate((xa, xb))]
    for copy in note_copies:
        copy.start()
    sources, targets = [], []
    for c in range(2 * chunks):
        emb, outs = ((images, (xa, xb)), (texts, (ya, yb)))[c // chunks]
        at = c % chunks * step
        sources.append([pltpu.make_async_copy(emb.at[pl.ds(at, step)], held.at[c], sems.at[0, c])])
        out = outs[at // half].at[pl.ds(at % half, step)]
        targets.append(pltpu.make_async_copy(done.at[c], out, sems.at[1, c]))

    def work(c):
        values = held[c].astype(jnp.float32)
        inverse = lax.rsqrt(jnp.sum(values * values, axis=-1, keepdims=True) + EPS)
        done[c] = (values * inverse).astype(jnp.bfloat16)

    chunked(2 * chunks, sources, targets, work)
    for copy in note_copies:
        copy.wait()


def normalize(images, texts, notes):
    rows, width = images.shape
    chunks = 4
    held = pltpu.VMEM((2 * chunks, rows // chunks, width), jnp.bfloat16)
    half = jax.ShapeDtypeStruct((rows // 2, width), jnp.bfloat16)
    noted = jax.ShapeDtypeStruct((rows // 2 + NOTES, width), jnp.bfloat16)
    return pl.pallas_call(
        functools.partial(normalize_kernel, chunks),
        in_specs=[ANY] * 3,
        out_specs=[ANY] * 4,
        out_shape=[noted, noted, half, half],
        scratch_shapes=[held, held, pltpu.SemaphoreType.DMA((2, 2 * chunks)), pltpu.SemaphoreType.DMA((2,))],
        **params(),
    )(images, texts, notes)


def when(condition, work):
    if condition is True:
        work()
    else:
        pl.when(condition)(work)


def block_copies(refs, offset, index, dst, sem):
    copies = []
    for part in range(2):
        if isinstance(index, int):
            local, inside = index % HALF, index // HALF == part
        else:
            local = jnp.clip(index - part * HALF, 0, HALF - 1)
            inside = (index >= part * HALF) & (index < (part + 1) * HALF)
        rows = pl.ds(local * ROWS if isinstance(index, int) else pl.multiple_of(local * ROWS, ROWS), ROWS)
        if inside is not False:
            copies.append((inside, pltpu.make_async_copy(refs[offset][part].at[rows], dst, sem)))
    return copies


def start_copies(live, copies):
    for inside, copy in copies:
        if inside is True or live is True:
            when(live if inside is True else inside, copy.start)
        else:
            when(live & inside, copy.start)


def split_refs(refs):
    return {offset: refs[2 * offset:2 * offset + 2] for offset in range(SIDE)}


N_REFS = 2 * SIDE


def columns(row):
    return jnp.transpose(jnp.broadcast_to(row, (128, ROWS)))


def coefficients(sims_ref, coef_ref, weight_ref, scale, offset, positive):
    def step(at, sums):
        loss_sum, coef_sum, dot_sum = sums
        rows = pl.ds(pl.multiple_of(at * CHUNK, CHUNK), CHUNK)
        sims = sims_ref[rows, :]
        logits = scale * sims + offset
        weight = jnp.concatenate([weight_ref[rows, :]] * (ROWS // 128), axis=1)
        scaled_weight = weight * scale
        if positive:
            row = lax.broadcasted_iota(jnp.int32, sims.shape, 0) + at * CHUNK
            col = lax.broadcasted_iota(jnp.int32, sims.shape, 1)
            diagonal = row == col
            logits = jnp.where(diagonal, -logits, logits)
            scaled_weight = jnp.where(diagonal, -scaled_weight, scaled_weight)
        power = jnp.exp(logits)
        one_more = 1.0 + power
        coef = scaled_weight * (power / one_more)
        loss = weight * jnp.log(one_more)
        coef_ref[rows, :] = coef.astype(jnp.bfloat16)

        def fold(value):
            return jnp.sum(value.reshape(CHUNK // 8, 8, ROWS), axis=0)

        return (loss_sum + fold(loss), coef_sum + fold(coef), dot_sum + fold(coef * sims))

    zero = jnp.zeros((8, ROWS), jnp.float32)
    return lax.fori_loop(0, ROWS // CHUNK, step, (zero, zero, zero))


def dot(lhs, rhs, dims):
    return lax.dot_general(lhs, rhs, (dims, ((), ())), preferred_element_type=jnp.float32)


NT = ((1,), (1,))
NN = ((1,), (0,))
TN = ((0,), (0,))


def read_entry(plans, place, slot):
    if slot[0] == POSITIVE:
        return slot[1], slot[1], True
    owner = (place[0] + slot[1]) % SIDE * SIDE + place[1]
    at = slot[0] * SLOT_NUMBERS + owner * 3
    return plans[at], plans[at + 1], plans[at + 2] > 0


def offsets_of(slot):
    return (0, 0) if slot[0] == POSITIVE else slot


def block_item(live, wanted, dst, sem, extra_copies, work):
    def start():
        for k, (refs, offset, index) in enumerate(wanted):
            start_copies(live, block_copies(refs, offset, index, dst[k], sem[k]))
        start_copies(live, [(True, copy) for copy in extra_copies])

    def wait():
        def waits():
            for k, (refs, offset, index) in enumerate(wanted):
                pltpu.make_async_copy(refs[0][0].at[pl.ds(0, ROWS)], dst[k], sem[k]).wait()
            for copy in extra_copies:
                copy.wait()

        when(live, waits)

    return start, wait, lambda: when(live, work)


def add_tile(acc, seen, index, tile):
    acc[index] = jnp.where(seen[index] > 0, acc[index], 0.0) + tile
    seen[index] = 1


def send_sums(acc, seen, staged, outs, sems, arrived=None):
    copies = []
    for b in range(BLK):
        total = jnp.where(seen[b] > 0, acc[b], 0.0)
        if arrived is not None:
            total = total + arrived[b].astype(jnp.float32)
        staged[b] = total.astype(staged.dtype)
        rows = pl.ds(b % HALF * ROWS, ROWS)
        copies.append(pltpu.make_async_copy(staged.at[b], outs[b // HALF].at[rows], sems.at[b]))
        copies[-1].start()
    return copies


def pairs_kernel(slots, summed, extras, n_sources, *refs):
    plans, place, scalars, image_rows = refs[0:4]
    at = 4
    xrefs, yrefs = split_refs(refs[at:at + N_REFS]), split_refs(refs[at + N_REFS:at + 2 * N_REFS])
    at += 2 * N_REFS
    sources = refs[at:at + n_sources]
    at += n_sources
    coef_out, stats_out = refs[at], refs[at + 1]
    at += 2
    grads = (refs[at:at + 2], refs[at + 2:at + 4]) if summed else ()
    at += 2 * len(grads)
    xbuf, ybuf, wbuf, sims, coefs, sems = refs[at:at + 6]
    if summed:
        acc, seen, staged, obuf, cbuf, esems, osems = refs[at + 6:at + 13]
    scale, offset = scalars[0], scalars[1]

    def slot_item(s, slot):
        (i, j), (p, q, live) = offsets_of(slot), read_entry(plans, place, slot)

        def work():
            wbuf[...] = columns(image_rows[pl.ds(i * BLK + p, 1), :])
            sims[...] = dot(xbuf[s], ybuf[s], NT)
            sums = coefficients(sims, coefs.at[s], wbuf, scale, offset, slot[0] == POSITIVE)
            for k in range(3):
                stats_out[k] += sums[k]
            pltpu.make_async_copy(coefs.at[s], coef_out.at[s], sems.at[2, s]).start()
            if summed and i == FAR:
                add_tile(acc.at[0], seen.at[0], p, dot(coefs[s], ybuf[s], NN))
            if summed and j == FAR:
                add_tile(acc.at[1], seen.at[1], q, dot(coefs[s], xbuf[s], TN))

        wanted = ((xrefs, i, p), (yrefs, j, q))
        return block_item(live, wanted, (xbuf.at[s], ybuf.at[s]), (sems.at[0, s], sems.at[1, s]), (), work)

    def extra_item(e, slot, source, index):
        p, q, live = read_entry(plans, place, slot)
        copy = pltpu.make_async_copy(sources[source].at[index], cbuf.at[e], esems.at[1, e])

        def work():
            add_tile(acc.at[0], seen.at[0], p, dot(cbuf[e], obuf[e], NN))

        return block_item(live, ((yrefs, slot[1], q),), (obuf.at[e],), (esems.at[0, e],), (copy,), work)

    copies = []

    def send(side):
        return lambda: copies.extend(send_sums(acc.at[side], seen.at[side], staged.at[side], grads[side], osems.at[side]))

    stats_out[...] = jnp.zeros_like(stats_out)
    items = [slot_item(s, slot) for s, slot in enumerate(slots)]
    if summed:
        for side in range(2):
            for b in range(BLK):
                seen[side, b] = 0
        nothing = lambda: None
        items[1:1] = [extra_item(e, *extra) for e, extra in enumerate(extras)] + [(nothing, nothing, send(0))]
        items.append((nothing, nothing, send(1)))
    pipelined(items, 5)
    for s, slot in enumerate(slots):
        live = read_entry(plans, place, slot)[2]
        when(live, pltpu.make_async_copy(coefs.at[s], coef_out.at[s], sems.at[2, s]).wait)
    for copy in copies:
        copy.wait()


def pairs(slots, extra_slots, sources, small, images, texts):
    width = texts[0].shape[1]
    total = len(slots)
    extras = tuple((slot, *COEF_AT[slot]) for slot in extra_slots)
    summed = len(extras) > 0
    out_shape = [
        jax.ShapeDtypeStruct((total, ROWS, ROWS), jnp.bfloat16),
        jax.ShapeDtypeStruct((3, 8, ROWS), jnp.float32),
    ]
    scratch = [
        pltpu.VMEM((total, ROWS, width), jnp.bfloat16),
        pltpu.VMEM((total, ROWS, width), jnp.bfloat16),
        pltpu.VMEM((ROWS, 128), jnp.float32),
        pltpu.VMEM((ROWS, ROWS), jnp.float32),
        pltpu.VMEM((total, ROWS, ROWS), jnp.bfloat16),
        pltpu.SemaphoreType.DMA((3, total)),
    ]
    if summed:
        out_shape += [jax.ShapeDtypeStruct((HALF * ROWS, width), jnp.bfloat16)] * 4
        scratch += [
            pltpu.VMEM((2, BLK, ROWS, width), jnp.float32),
            pltpu.SMEM((2, BLK), jnp.int32),
            pltpu.VMEM((2, BLK, ROWS, width), jnp.bfloat16),
            pltpu.VMEM((len(extras), ROWS, width), jnp.bfloat16),
            pltpu.VMEM((len(extras), ROWS, ROWS), jnp.bfloat16),
            pltpu.SemaphoreType.DMA((2, len(extras))),
            pltpu.SemaphoreType.DMA((2, BLK)),
        ]
    return pl.pallas_call(
        functools.partial(pairs_kernel, slots, summed, extras, len(sources)),
        in_specs=[SMEM, SMEM, SMEM, WHOLE] + [ANY] * (2 * N_REFS + len(sources)),
        out_specs=[ANY, WHOLE] + [ANY] * (len(out_shape) - 2),
        out_shape=out_shape,
        scratch_shapes=scratch,
        **params(),
    )(*small, *images, *texts, *sources)


def grads_kernel(axis, groups, n_arrived, *refs):
    plans, place = refs[0:2]
    other = split_refs(refs[2:2 + N_REFS])
    at = 2 + N_REFS
    coefs = refs[at:at + len(GROUPS)]
    arrived = refs[at + len(GROUPS):at + len(GROUPS) + n_arrived]
    at += len(GROUPS) + n_arrived
    outs = refs[at:at + 2 * len(groups)]
    buf, cbuf, acc, seen, staged, sems, osems = refs[at + 2 * len(groups):at + 2 * len(groups) + 7]
    mine = 0 if axis == "x" else 1
    dims = NN if axis == "x" else TN
    items, copies, arrivals = [], [], []
    if n_arrived:
        abuf, asems = refs[-2:]
        for b in range(BLK):
            rows = pl.ds(b % HALF * ROWS, ROWS)
            arrivals.append(pltpu.make_async_copy(arrived[b // HALF].at[rows], abuf.at[b], asems.at[b]))

    def slot_item(at, group, last, slot, source, index):
        entry = read_entry(plans, place, slot)
        copy = pltpu.make_async_copy(coefs[source].at[index], cbuf.at[at], sems.at[1, at])

        def work():
            add_tile(acc.at[group], seen.at[group], entry[mine], dot(cbuf[at], buf[at], dims))

        wanted = ((other, offsets_of(slot)[1 - mine], entry[1 - mine]),)
        start, wait, run = block_item(entry[2], wanted, (buf.at[at],), (sems.at[0, at],), (copy,), work)

        def run_and_send():
            run()
            if last:
                for arrival in arrivals:
                    arrival.wait()
                copies.extend(send_sums(
                    acc.at[group], seen.at[group], staged.at[group], outs[2 * group:2 * group + 2], osems.at[group],
                    abuf if n_arrived else None))

        return start, wait, run_and_send

    for group, entries in enumerate(groups):
        for b in range(BLK):
            seen[group, b] = 0
        for entry in entries:
            items.append(slot_item(len(items), group, entry is entries[-1], *entry))
    for arrival in arrivals:
        arrival.start()
    pipelined(items, 5)
    for copy in copies:
        copy.wait()


def grads(axis, offsets, with_positive, small, blocks, coefs, arrived=()):
    width = blocks[0].shape[1]
    groups = []
    for offset in offsets:
        group = []
        for neighbour in (0, 1, 3, 2):
            slot = (offset, neighbour) if axis == "x" else (neighbour, offset)
            if slot != (0, 0):
                group.append((slot, *COEF_AT[slot]))
        if with_positive:
            group += [((POSITIVE, b), 0, len(EARLY) + b) for b in range(BLK)]
        groups.append(tuple(group))
    total = sum(len(group) for group in groups)
    scratch = [
        pltpu.VMEM((total, ROWS, width), jnp.bfloat16),
        pltpu.VMEM((total, ROWS, ROWS), jnp.bfloat16),
        pltpu.VMEM((len(groups), BLK, ROWS, width), jnp.float32),
        pltpu.SMEM((len(groups), BLK), jnp.int32),
        pltpu.VMEM((len(groups), BLK, ROWS, width), jnp.bfloat16),
        pltpu.SemaphoreType.DMA((2, total)),
        pltpu.SemaphoreType.DMA((len(groups), BLK)),
    ]
    if arrived:
        scratch += [pltpu.VMEM((BLK, ROWS, width), jnp.bfloat16), pltpu.SemaphoreType.DMA((BLK,))]
    return pl.pallas_call(
        functools.partial(grads_kernel, axis, tuple(groups), len(arrived)),
        in_specs=[SMEM, SMEM] + [ANY] * (N_REFS + len(GROUPS) + len(arrived)),
        out_specs=[ANY] * (2 * len(groups)),
        out_shape=[jax.ShapeDtypeStruct((HALF * ROWS, width), jnp.bfloat16)] * (2 * len(groups)),
        scratch_shapes=scratch,
        **params(),
    )(*small[:2], *blocks, *coefs, *arrived)


def finish_kernel(chunks, emb, own_a, own_b, last_a, last_b, out, embs, owns, lasts, done, sems):
    half = own_a.shape[0]
    step = 2 * half // chunks
    sources, targets = [], []
    for c in range(chunks):
        own, last = ((own_a, last_a), (own_b, last_b))[c * step // half]
        rows, of_whole = pl.ds(c * step % half, step), pl.ds(c * step, step)
        pieces = ((emb, of_whole, embs), (own, rows, owns), (last, rows, lasts))
        sources.append([
            pltpu.make_async_copy(ref.at[at], held.at[c], sems.at[k, c]) for k, (ref, at, held) in enumerate(pieces)])
        targets.append(pltpu.make_async_copy(done.at[c], out.at[of_whole], sems.at[3, c]))

    def work(c):
        values = embs[c].astype(jnp.float32)
        inverse = lax.rsqrt(jnp.sum(values * values, axis=-1, keepdims=True) + EPS)
        total = owns[c].astype(jnp.float32) + lasts[c].astype(jnp.float32)
        inner = jnp.sum(values * total, axis=-1, keepdims=True) * (inverse * inverse)
        done[c] = (inverse * (total - values * inner)).astype(jnp.bfloat16)

    chunked(chunks, sources, targets, work)


def finish(emb, own, last):
    rows, width = emb.shape
    chunks = 8
    held = pltpu.VMEM((chunks, rows // chunks, width), jnp.bfloat16)
    return pl.pallas_call(
        functools.partial(finish_kernel, chunks),
        in_specs=[ANY] * 5,
        out_specs=ANY,
        out_shape=jax.ShapeDtypeStruct(emb.shape, jnp.bfloat16),
        scratch_shapes=[held] * 4 + [pltpu.SemaphoreType.DMA((4, chunks))],
        **params(),
    )(emb, *own, *last)


def shift(value, axis, by):
    pairs_of = []
    for y in range(SIDE):
        for x in range(SIDE):
            to = (y * SIDE + (x + by) % SIDE) if axis == "x" else ((y + by) % SIDE * SIDE + x)
            pairs_of.append((y * SIDE + x, to))
    return lax.ppermute(value, "txt", pairs_of)


def after(values, done):
    out = lax.optimization_barrier(tuple(values) + tuple(done))
    return out[:len(values)]


def both_ways(axis, forward, backward, done=()):
    if done:
        forward, backward = after((forward, backward), done)
    return shift(forward, axis, 1), shift(backward, axis, -1)


def add_partner(value, axis, bit):
    size = lax.axis_size(axis)
    return value + lax.ppermute(value, axis, [(i, i ^ bit) for i in range(size)])


def join(ours, arrived):
    return (ours.astype(jnp.float32) + arrived.astype(jnp.float32)).astype(jnp.bfloat16)


def per_device(image_emb, text_emb, row_weight, log_scale, bias, pair_slots):
    width = image_emb.shape[1]
    half = HALF * ROWS
    scale = jnp.exp(log_scale[0])
    scalars = jnp.stack([scale, bias[0]])
    weights = jnp.pad(row_weight.reshape(BLK, ROWS), ((0, 0), (0, width - ROWS)))
    plan = jnp.pad(pair_slots.astype(jnp.bfloat16).reshape(1, -1), ((0, NOTES - BLK - 1), (0, width - SLOT_NUMBERS)))
    xa, xb, ya, yb = normalize(image_emb, text_emb, jnp.concatenate([weights, plan]))

    x1 = both_ways("x", xa, xb)
    y1 = both_ways("y", ya, yb)
    x2 = both_ways("x", *x1, x1)
    y2 = both_ways("y", yb, ya, y1)
    x3 = both_ways("x", xb, xa, x2)
    y3 = both_ways("y", *y1, y2)
    y_next, y_prev = (y2[1], y1[1]), (y1[0], y2[0])
    own_x, own_y = (xa, xb), (ya, yb)

    notes = [message[half:half + BLK + 1, :ROWS].astype(jnp.float32) for message in (xa, x1[1], x2[0], x1[0])]
    weight_rows = jnp.concatenate([note[:BLK] for note in notes])
    plans = jnp.concatenate([note[BLK, :SLOT_NUMBERS] for note in notes]).astype(jnp.int32)
    me = lax.axis_index("txt")
    place = jnp.stack([me // SIDE, me % SIDE]).astype(jnp.int32)
    small = (plans, place, scalars, weight_rows)

    early_x = (*own_x, *own_x, *x2, *own_x)
    early_y = (*own_y, *y_next, *own_y, *y_prev)
    positives = tuple((POSITIVE, b) for b in range(BLK))
    early, early_stats = pairs(EARLY + positives, (), (), small, early_x, early_y)
    early, early_stats, *arrived = lax.optimization_barrier((early, early_stats, *x3, *y3))
    x3, y3 = arrived[:2], arrived[2:]
    x_next, x_prev = (x3[1], x1[1]), (x1[0], x3[0])
    images = (*own_x, *x_next, *x2, *x_prev)
    texts = (*own_y, *y_next, *y3, *y_prev)

    to_sum = ((FAR, 0), (FAR, 1), (FAR, 3))
    opposite, opposite_stats, *far = pairs(OPPOSITE, to_sum, (early,), small, images, texts)
    x4 = both_ways("x", *far[:2])
    y4 = both_ways("y", *far[2:])
    late, late_stats = pairs(LATE, (), (), after(small, far), images, texts)
    coefs = (early, opposite, late)
    dx_next_a, dx_next_b, dx_prev_a, dx_prev_b = grads("x", (1, 3), False, small, texts, coefs)
    dy_next_a, dy_next_b, dy_prev_a, dy_prev_b = grads("y", (1, 3), False, small, images, coefs)

    x5 = both_ways("x", dx_next_b, dx_prev_a, x4)
    y5 = both_ways("y", dy_next_b, dy_prev_a, y4)
    joined_x = join(dx_next_a, x4[0]), join(dx_prev_b, x4[1])
    joined_y = join(dy_next_a, y4[0]), join(dy_prev_b, y4[1])

    sums = jnp.sum((early_stats + opposite_stats + late_stats).reshape(3, -1), axis=1)
    stats = jnp.stack([sums[0], sums[2], sums[1] / scale])
    (stats,) = after((stats,), (*x4, *y4))
    for bit in (1, 2, 4):
        stats = add_partner(stats, "img", bit)
    stats = add_partner(stats, "txt", 1)
    *x5, stats = lax.optimization_barrier((*x5, stats))
    x6 = both_ways("x", *joined_x, x5)
    y6 = both_ways("y", *joined_y, y5)
    own_small = after(small, (*x5, *y5))
    dx_own = grads("x", (0,), True, own_small, texts, coefs, (x5[1], x5[0]))
    dy_own = grads("y", (0,), True, own_small, images, coefs, (y5[1], y5[0]))
    stats = add_partner(stats, "txt", 2)
    x6 = after(x6, (*dx_own, *dy_own))
    y6 = after(y6, (*dx_own, *dy_own))
    (stats,) = after((stats,), (*x6, *y6))
    stats = add_partner(stats, "txt", SIDE)
    grad_image = finish(image_emb, dx_own, x6)
    y6 = after(y6, (stats,))
    stats = add_partner(stats, "txt", 2 * SIDE)
    grad_text = finish(text_emb, dy_own, y6)
    count = BLK * ROWS * lax.axis_size("img") * lax.axis_size("txt")
    return (grad_image, grad_text, stats / count)


def solution(mesh):
    return jax.shard_map(
        per_device,
        mesh=mesh,
        in_specs=(
            P(("img", "txt"), None),
            P(("img", "txt"), None),
            P(("img", "txt")),
            P(),
            P(),
            P(("img", "txt"), None),
        ),
        out_specs=(P(("img", "txt"), None), P(("img", "txt"), None), P()),
        check_vma=False,
    )
```

```python
import functools

import jax
import jax.numpy as jnp
from jax import lax
from jax.experimental import pallas as pl
from jax.experimental.pallas import tpu as pltpu
from jax.sharding import PartitionSpec as P

ROWS = 384
BLK = 4
SIDE = 4
HALF = BLK // 2
EPS = 1e-06
VMEM = 60 * 1024 * 1024
CHUNK = 48

FAR = 2
EARLY = ((0, 1), (0, 3), (FAR, 0), (FAR, 1), (FAR, 3))
OPPOSITE = ((FAR, FAR), (0, FAR), (1, FAR), (3, FAR))
LATE = tuple((i, j) for i in (1, 3) for j in (0, 1, 3))
GROUPS = (EARLY, OPPOSITE, LATE)
COEF_AT = {slot: (source, known.index(slot)) for source, known in enumerate(GROUPS) for slot in known}
POSITIVE = "positive"
SLOT_NUMBERS = 3 * SIDE * SIDE
NOTES = 16
ANY = pl.BlockSpec(memory_space=pl.ANY)
SMEM = pl.BlockSpec(memory_space=pltpu.SMEM)
WHOLE = pl.BlockSpec(memory_space=pltpu.VMEM)


def params():
    return dict(
        compiler_params=pltpu.CompilerParams(vmem_limit_bytes=VMEM),
        cost_estimate=pl.CostEstimate(flops=1000, bytes_accessed=1000, transcendentals=0),
    )


def pipelined(items, ahead):
    for start, _, _ in items[:ahead]:
        start()
    for at, (_, wait, work) in enumerate(items):
        wait()
        if at + ahead < len(items):
            items[at + ahead][0]()
        work()


def chunked(chunks, sources, targets, work):
    def item(c):
        def start():
            for copy in sources[c]:
                copy.start()

        def wait():
            for copy in sources[c]:
                copy.wait()

        def run():
            work(c)
            targets[c].start()

        return start, wait, run

    pipelined([item(c) for c in range(chunks)], chunks)
    for copy in targets:
        copy.wait()


def normalize_kernel(chunks, images, texts, notes, xa, xb, ya, yb, held, done, sems, note_sems):
    half = images.shape[0] // 2
    step = 2 * half // chunks
    note_copies = [
        pltpu.make_async_copy(notes, out.at[pl.ds(half, NOTES)], note_sems.at[k]) for k, out in enumerate((xa, xb))]
    for copy in note_copies:
        copy.start()
    sources, targets = [], []
    for c in range(2 * chunks):
        emb, outs = ((images, (xa, xb)), (texts, (ya, yb)))[c // chunks]
        at = c % chunks * step
        sources.append([pltpu.make_async_copy(emb.at[pl.ds(at, step)], held.at[c], sems.at[0, c])])
        out = outs[at // half].at[pl.ds(at % half, step)]
        targets.append(pltpu.make_async_copy(done.at[c], out, sems.at[1, c]))

    def work(c):
        values = held[c].astype(jnp.float32)
        inverse = lax.rsqrt(jnp.sum(values * values, axis=-1, keepdims=True) + EPS)
        done[c] = (values * inverse).astype(jnp.bfloat16)

    chunked(2 * chunks, sources, targets, work)
    for copy in note_copies:
        copy.wait()


def normalize(images, texts, notes):
    rows, width = images.shape
    chunks = 4
    held = pltpu.VMEM((2 * chunks, rows // chunks, width), jnp.bfloat16)
    half = jax.ShapeDtypeStruct((rows // 2, width), jnp.bfloat16)
    noted = jax.ShapeDtypeStruct((rows // 2 + NOTES, width), jnp.bfloat16)
    return pl.pallas_call(
        functools.partial(normalize_kernel, chunks),
        in_specs=[ANY] * 3,
        out_specs=[ANY] * 4,
        out_shape=[noted, noted, half, half],
        scratch_shapes=[held, held, pltpu.SemaphoreType.DMA((2, 2 * chunks)), pltpu.SemaphoreType.DMA((2,))],
        **params(),
    )(images, texts, notes)


def when(condition, work):
    if condition is True:
        work()
    else:
        pl.when(condition)(work)


def block_copies(refs, offset, index, dst, sem):
    copies = []
    for part in range(2):
        if isinstance(index, int):
            local, inside = index % HALF, index // HALF == part
        else:
            local = jnp.clip(index - part * HALF, 0, HALF - 1)
            inside = (index >= part * HALF) & (index < (part + 1) * HALF)
        rows = pl.ds(local * ROWS if isinstance(index, int) else pl.multiple_of(local * ROWS, ROWS), ROWS)
        if inside is not False:
            copies.append((inside, pltpu.make_async_copy(refs[offset][part].at[rows], dst, sem)))
    return copies


def start_copies(live, copies):
    for inside, copy in copies:
        if inside is True or live is True:
            when(live if inside is True else inside, copy.start)
        else:
            when(live & inside, copy.start)


def split_refs(refs):
    return {offset: refs[2 * offset:2 * offset + 2] for offset in range(SIDE)}


N_REFS = 2 * SIDE


def columns(row):
    return jnp.transpose(jnp.broadcast_to(row, (128, ROWS)))


def coefficients(sims_ref, coef_ref, weight_ref, scale, offset, positive):
    def step(at, sums):
        loss_sum, coef_sum, dot_sum = sums
        rows = pl.ds(pl.multiple_of(at * CHUNK, CHUNK), CHUNK)
        sims = sims_ref[rows, :]
        logits = scale * sims + offset
        weight = jnp.concatenate([weight_ref[rows, :]] * (ROWS // 128), axis=1)
        scaled_weight = weight * scale
        if positive:
            row = lax.broadcasted_iota(jnp.int32, sims.shape, 0) + at * CHUNK
            col = lax.broadcasted_iota(jnp.int32, sims.shape, 1)
            diagonal = row == col
            logits = jnp.where(diagonal, -logits, logits)
            scaled_weight = jnp.where(diagonal, -scaled_weight, scaled_weight)
        power = jnp.exp(logits)
        one_more = 1.0 + power
        coef = scaled_weight * (power / one_more)
        loss = weight * jnp.log(one_more)
        coef_ref[rows, :] = coef.astype(jnp.bfloat16)

        def fold(value):
            return jnp.sum(value.reshape(CHUNK // 8, 8, ROWS), axis=0)

        return (loss_sum + fold(loss), coef_sum + fold(coef), dot_sum + fold(coef * sims))

    zero = jnp.zeros((8, ROWS), jnp.float32)
    return lax.fori_loop(0, ROWS // CHUNK, step, (zero, zero, zero), unroll=True)


def dot(lhs, rhs, dims):
    return lax.dot_general(lhs, rhs, (dims, ((), ())), preferred_element_type=jnp.float32)


NT = ((1,), (1,))
NN = ((1,), (0,))
TN = ((0,), (0,))


def read_entry(plans, place, slot):
    if slot[0] == POSITIVE:
        return slot[1], slot[1], True
    owner = (place[0] + slot[1]) % SIDE * SIDE + place[1]
    at = slot[0] * SLOT_NUMBERS + owner * 3
    return plans[at], plans[at + 1], plans[at + 2] > 0


def offsets_of(slot):
    return (0, 0) if slot[0] == POSITIVE else slot


def block_item(live, wanted, dst, sem, extra_copies, work):
    def start():
        for k, (refs, offset, index) in enumerate(wanted):
            start_copies(live, block_copies(refs, offset, index, dst[k], sem[k]))
        start_copies(live, [(True, copy) for copy in extra_copies])

    def wait():
        def waits():
            for k, (refs, offset, index) in enumerate(wanted):
                pltpu.make_async_copy(refs[0][0].at[pl.ds(0, ROWS)], dst[k], sem[k]).wait()
            for copy in extra_copies:
                copy.wait()

        when(live, waits)

    return start, wait, lambda: when(live, work)


def add_tile(acc, seen, index, tile):
    acc[index] = jnp.where(seen[index] > 0, acc[index], 0.0) + tile
    seen[index] = 1


def send_sums(acc, seen, staged, outs, sems, arrived=None):
    copies = []
    for b in range(BLK):
        total = jnp.where(seen[b] > 0, acc[b], 0.0)
        if arrived is not None:
            total = total + arrived[b].astype(jnp.float32)
        staged[b] = total.astype(staged.dtype)
        rows = pl.ds(b % HALF * ROWS, ROWS)
        copies.append(pltpu.make_async_copy(staged.at[b], outs[b // HALF].at[rows], sems.at[b]))
        copies[-1].start()
    return copies


def arrivals_of(parts, buf, sems):
    return [
        pltpu.make_async_copy(parts[b // HALF].at[pl.ds(b % HALF * ROWS, ROWS)], buf.at[b], sems.at[b])
        for b in range(BLK)]


def pairs_kernel(slots, sides, n_arrived, *refs):
    plans, place, scalars, image_rows = refs[0:4]
    at = 4
    xrefs, yrefs = split_refs(refs[at:at + N_REFS]), split_refs(refs[at + N_REFS:at + 2 * N_REFS])
    at += 2 * N_REFS
    arrived = refs[at:at + n_arrived]
    at += n_arrived
    coef_out, stats_out = refs[at], refs[at + 1]
    at += 2
    outs = refs[at:at + 2 * len(sides)]
    at += len(outs)
    xbuf, ybuf, wbuf, sims, coefs, sems, acc, seen, staged, osems = refs[at:at + 10]
    arrivals = arrivals_of(arrived, *refs[-2:]) if n_arrived else []
    scale, offset = scalars[0], scalars[1]
    copies = []

    def slot_item(s, slot):
        (i, j), (p, q, live) = offsets_of(slot), read_entry(plans, place, slot)

        def work():
            wbuf[...] = columns(image_rows[pl.ds(i * BLK + p, 1), :])
            for part in range(2):
                rows = pl.ds(part * (ROWS // 2), ROWS // 2)
                sims[rows, :] = dot(xbuf[s, rows, :], ybuf[s], NT)
            sums = coefficients(sims, coefs.at[s], wbuf, scale, offset, slot[0] == POSITIVE)
            for k in range(3):
                stats_out[k] += sums[k]
            pltpu.make_async_copy(coefs.at[s], coef_out.at[s], sems.at[2, s]).start()
            if "x" in sides and i == FAR:
                add_tile(acc.at[0], seen.at[0], p, dot(coefs[s], ybuf[s], NN))
            if "y" in sides and j == FAR:
                add_tile(acc.at[1], seen.at[1], q, dot(coefs[s], xbuf[s], TN))

        wanted = ((xrefs, i, p), (yrefs, j, q))
        return block_item(live, wanted, (xbuf.at[s], ybuf.at[s]), (sems.at[0, s], sems.at[1, s]), (), work)

    def send(side):
        for arrival in arrivals if side == 0 else ():
            arrival.wait()
        copies.extend(send_sums(
            acc.at[side], seen.at[side], staged.at[side], outs[2 * side:2 * side + 2], osems.at[side],
            refs[-2] if arrivals and side == 0 else None))

    stats_out[...] = jnp.zeros_like(stats_out)
    for side in range(len(sides)):
        for b in range(BLK):
            seen[side, b] = 0
    items = [slot_item(s, slot) for s, slot in enumerate(slots)]
    last = {"x": max([s for s, slot in enumerate(slots) if slot[0] == FAR], default=0), "y": len(slots) - 1}
    for side in reversed(range(len(sides))):
        at = last[sides[side]] + 1
        items.insert(at, (lambda: None, lambda: None, functools.partial(send, side)))
    items.insert(1, (lambda: [arrival.start() for arrival in arrivals], lambda: None, lambda: None))
    pipelined(items, 3)
    for s, slot in enumerate(slots):
        live = read_entry(plans, place, slot)[2]
        when(live, pltpu.make_async_copy(coefs.at[s], coef_out.at[s], sems.at[2, s]).wait)
    for copy in copies:
        copy.wait()


def pairs(slots, sides, arrived, small, images, texts):
    width = texts[0].shape[1]
    total = len(slots)
    held = max(len(sides), 1)
    blocks = (held, BLK, ROWS, width) if sides else (1, 1, 8, 128)
    out_shape = [
        jax.ShapeDtypeStruct((total, ROWS, ROWS), jnp.bfloat16),
        jax.ShapeDtypeStruct((3, 8, ROWS), jnp.float32),
    ] + [jax.ShapeDtypeStruct((HALF * ROWS, width), jnp.bfloat16)] * (2 * len(sides))
    scratch = [
        pltpu.VMEM((total, ROWS, width), jnp.bfloat16),
        pltpu.VMEM((total, ROWS, width), jnp.bfloat16),
        pltpu.VMEM((ROWS, 128), jnp.float32),
        pltpu.VMEM((ROWS, ROWS), jnp.float32),
        pltpu.VMEM((total, ROWS, ROWS), jnp.bfloat16),
        pltpu.SemaphoreType.DMA((3, total)),
        pltpu.VMEM(blocks, jnp.float32),
        pltpu.SMEM((held, BLK), jnp.int32),
        pltpu.VMEM(blocks, jnp.bfloat16),
        pltpu.SemaphoreType.DMA((held, BLK)),
    ]
    if arrived:
        scratch += [pltpu.VMEM((BLK, ROWS, width), jnp.bfloat16), pltpu.SemaphoreType.DMA((BLK,))]
    return pl.pallas_call(
        functools.partial(pairs_kernel, slots, sides, len(arrived)),
        in_specs=[SMEM, SMEM, SMEM, WHOLE] + [ANY] * (2 * N_REFS + len(arrived)),
        out_specs=[ANY, WHOLE] + [ANY] * (len(out_shape) - 2),
        out_shape=out_shape,
        scratch_shapes=scratch,
        **params(),
    )(*small, *images, *texts, *arrived)


def grads_kernel(axis, groups, n_arrived, *refs):
    plans, place = refs[0:2]
    other = split_refs(refs[2:2 + N_REFS])
    at = 2 + N_REFS
    coefs = refs[at:at + len(GROUPS)]
    arrived = refs[at + len(GROUPS):at + len(GROUPS) + n_arrived]
    at += len(GROUPS) + n_arrived
    outs = refs[at:at + 2 * len(groups)]
    buf, cbuf, acc, seen, staged, sems, osems = refs[at + 2 * len(groups):at + 2 * len(groups) + 7]
    mine = 0 if axis == "x" else 1
    dims = NN if axis == "x" else TN
    items, copies, arrivals = [], [], []
    if n_arrived:
        abuf, asems = refs[-2:]
        arrivals = arrivals_of(arrived, abuf, asems)

    def slot_item(at, group, last, slot, source, index):
        entry = read_entry(plans, place, slot)
        copy = pltpu.make_async_copy(coefs[source].at[index], cbuf.at[at], sems.at[1, at])

        def work():
            add_tile(acc.at[group], seen.at[group], entry[mine], dot(cbuf[at], buf[at], dims))

        wanted = ((other, offsets_of(slot)[1 - mine], entry[1 - mine]),)
        start, wait, run = block_item(entry[2], wanted, (buf.at[at],), (sems.at[0, at],), (copy,), work)

        def run_and_send():
            run()
            if last:
                for arrival in arrivals:
                    arrival.wait()
                copies.extend(send_sums(
                    acc.at[group], seen.at[group], staged.at[group], outs[2 * group:2 * group + 2], osems.at[group],
                    abuf if n_arrived else None))

        return start, wait, run_and_send

    for group, entries in enumerate(groups):
        for b in range(BLK):
            seen[group, b] = 0
        for entry in entries:
            items.append(slot_item(len(items), group, entry is entries[-1], *entry))
    for arrival in arrivals:
        arrival.start()
    pipelined(items, 5)
    for copy in copies:
        copy.wait()


def grads(axis, offsets, with_positive, small, blocks, coefs, arrived=()):
    width = blocks[0].shape[1]
    groups = []
    for offset in offsets:
        group = []
        for neighbour in (0, 1, 3, 2):
            slot = (offset, neighbour) if axis == "x" else (neighbour, offset)
            if slot != (0, 0):
                group.append((slot, *COEF_AT[slot]))
        if with_positive:
            group += [((POSITIVE, b), 0, len(EARLY) + b) for b in range(BLK)]
        groups.append(tuple(group))
    total = sum(len(group) for group in groups)
    scratch = [
        pltpu.VMEM((total, ROWS, width), jnp.bfloat16),
        pltpu.VMEM((total, ROWS, ROWS), jnp.bfloat16),
        pltpu.VMEM((len(groups), BLK, ROWS, width), jnp.float32),
        pltpu.SMEM((len(groups), BLK), jnp.int32),
        pltpu.VMEM((len(groups), BLK, ROWS, width), jnp.bfloat16),
        pltpu.SemaphoreType.DMA((2, total)),
        pltpu.SemaphoreType.DMA((len(groups), BLK)),
    ]
    if arrived:
        scratch += [pltpu.VMEM((BLK, ROWS, width), jnp.bfloat16), pltpu.SemaphoreType.DMA((BLK,))]
    return pl.pallas_call(
        functools.partial(grads_kernel, axis, tuple(groups), len(arrived)),
        in_specs=[SMEM, SMEM] + [ANY] * (N_REFS + len(GROUPS) + len(arrived)),
        out_specs=[ANY] * (2 * len(groups)),
        out_shape=[jax.ShapeDtypeStruct((HALF * ROWS, width), jnp.bfloat16)] * (2 * len(groups)),
        scratch_shapes=scratch,
        **params(),
    )(*small[:2], *blocks, *coefs, *arrived)


def finish_kernel(chunks, emb, own_a, own_b, last_a, last_b, out, embs, owns, lasts, done, sems):
    half = own_a.shape[0]
    step = 2 * half // chunks
    sources, targets = [], []
    for c in range(chunks):
        own, last = ((own_a, last_a), (own_b, last_b))[c * step // half]
        rows, of_whole = pl.ds(c * step % half, step), pl.ds(c * step, step)
        pieces = ((emb, of_whole, embs), (own, rows, owns), (last, rows, lasts))
        sources.append([
            pltpu.make_async_copy(ref.at[at], held.at[c], sems.at[k, c]) for k, (ref, at, held) in enumerate(pieces)])
        targets.append(pltpu.make_async_copy(done.at[c], out.at[of_whole], sems.at[3, c]))

    def work(c):
        values = embs[c].astype(jnp.float32)
        inverse = lax.rsqrt(jnp.sum(values * values, axis=-1, keepdims=True) + EPS)
        total = owns[c].astype(jnp.float32) + lasts[c].astype(jnp.float32)
        inner = jnp.sum(values * total, axis=-1, keepdims=True) * (inverse * inverse)
        done[c] = (inverse * (total - values * inner)).astype(jnp.bfloat16)

    chunked(chunks, sources, targets, work)


def finish(emb, own, last):
    rows, width = emb.shape
    chunks = 8
    held = pltpu.VMEM((chunks, rows // chunks, width), jnp.bfloat16)
    return pl.pallas_call(
        functools.partial(finish_kernel, chunks),
        in_specs=[ANY] * 5,
        out_specs=ANY,
        out_shape=jax.ShapeDtypeStruct(emb.shape, jnp.bfloat16),
        scratch_shapes=[held] * 4 + [pltpu.SemaphoreType.DMA((4, chunks))],
        **params(),
    )(emb, *own, *last)


def shift(value, axis, by):
    pairs_of = []
    for y in range(SIDE):
        for x in range(SIDE):
            to = (y * SIDE + (x + by) % SIDE) if axis == "x" else ((y + by) % SIDE * SIDE + x)
            pairs_of.append((y * SIDE + x, to))
    return lax.ppermute(value, "txt", pairs_of)


def after(values, done):
    out = lax.optimization_barrier(tuple(values) + tuple(done))
    return out[:len(values)]


def both_ways(axis, forward, backward, done=()):
    if done:
        (forward,), (backward,) = after((forward,), done[:1]), after((backward,), done[1:])
    return shift(forward, axis, 1), shift(backward, axis, -1)


def add_partner(value, axis, bit):
    size = lax.axis_size(axis)
    return value + lax.ppermute(value, axis, [(i, i ^ bit) for i in range(size)])


def join(ours, arrived):
    return (ours.astype(jnp.float32) + arrived.astype(jnp.float32)).astype(jnp.bfloat16)


def per_device(image_emb, text_emb, row_weight, log_scale, bias, pair_slots):
    width = image_emb.shape[1]
    half = HALF * ROWS
    scale = jnp.exp(log_scale[0])
    scalars = jnp.stack([scale, bias[0]])
    weights = jnp.pad(row_weight.reshape(BLK, ROWS), ((0, 0), (0, width - ROWS)))
    plan = jnp.pad(pair_slots.astype(jnp.bfloat16).reshape(1, -1), ((0, NOTES - BLK - 1), (0, width - SLOT_NUMBERS)))
    xa, xb, ya, yb = normalize(image_emb, text_emb, jnp.concatenate([weights, plan]))

    x1 = both_ways("x", xa, xb)
    y1 = both_ways("y", ya, yb)
    x2 = both_ways("x", *x1)
    y2 = both_ways("y", yb, ya, y1)
    x3 = both_ways("x", xb, xa, x2)
    y3 = both_ways("y", *y1, y2)
    y_next, y_prev = (y2[1], y1[1]), (y1[0], y2[0])
    own_x, own_y = (xa, xb), (ya, yb)

    notes = [message[half:half + BLK + 1, :ROWS].astype(jnp.float32) for message in (xa, x1[1], x2[0], x1[0])]
    weight_rows = jnp.concatenate([note[:BLK] for note in notes])
    plans = jnp.concatenate([note[BLK, :SLOT_NUMBERS] for note in notes]).astype(jnp.int32)
    me = lax.axis_index("txt")
    place = jnp.stack([me // SIDE, me % SIDE]).astype(jnp.int32)
    small = (plans, place, scalars, weight_rows)

    early_x = (*own_x, *own_x, *x2, *own_x)
    early_y = (*own_y, *y_next, *own_y, *y_prev)
    positives = tuple((POSITIVE, b) for b in range(BLK))
    early, early_stats, *dx_far = pairs(EARLY + positives, ("x",), (), small, early_x, early_y)
    early, early_stats, *arrived = lax.optimization_barrier((early, early_stats, *x3, *y3))
    x3, y3 = arrived[:2], arrived[2:]
    x_next, x_prev = (x3[1], x1[1]), (x1[0], x3[0])
    images = (*own_x, *x_next, *x2, *x_prev)
    texts = (*own_y, *y_next, *y3, *y_prev)

    opposite, opposite_stats, *far = pairs(OPPOSITE, ("x", "y"), tuple(dx_far), small, images, texts)
    x4 = both_ways("x", *far[:2])
    y4 = both_ways("y", *far[2:])
    late, late_stats = pairs(LATE, (), (), after(small, far), images, texts)
    coefs = (early, opposite, late)
    dx_next_a, dx_next_b, dx_prev_a, dx_prev_b = grads("x", (1, 3), False, small, texts, coefs)
    dy_next_a, dy_next_b, dy_prev_a, dy_prev_b = grads("y", (1, 3), False, small, images, coefs)

    sums = jnp.sum((early_stats + opposite_stats + late_stats).reshape(3, -1), axis=1)
    stats = jnp.stack([sums[0], sums[2], sums[1] / scale])
    stats = add_partner(stats, "txt", 1)
    *x4, stats = lax.optimization_barrier((*x4, stats))
    x5 = both_ways("x", dx_next_b, dx_prev_a, x4)
    y5 = both_ways("y", dy_next_b, dy_prev_a, y4)
    joined_x = join(dx_next_a, x4[0]), join(dx_prev_b, x4[1])
    joined_y = join(dy_next_a, y4[0]), join(dy_prev_b, y4[1])
    for bit in (1, 2, 4):
        stats = add_partner(stats, "img", bit)
    stats = add_partner(stats, "txt", 2)
    *x5, stats = lax.optimization_barrier((*x5, stats))
    x6 = both_ways("x", *joined_x, x5)
    y6 = both_ways("y", *joined_y, y5)
    own_small = after(small, (*x5, *y5))
    dx_own = grads("x", (0,), True, own_small, texts, coefs, (x5[1], x5[0]))
    dy_own = grads("y", (0,), True, own_small, images, coefs, (y5[1], y5[0]))
    stats = add_partner(stats, "txt", SIDE)
    x6 = after(x6, (*dx_own, *dy_own))
    y6 = after(y6, (*dx_own, *dy_own))
    stats = add_partner(stats, "txt", 2 * SIDE)
    x6 = after(x6, (stats,))
    grad_image = finish(image_emb, dx_own, x6)
    grad_text = finish(text_emb, dy_own, y6)
    count = BLK * ROWS * lax.axis_size("img") * lax.axis_size("txt")
    return (grad_image, grad_text, stats / count)


def solution(mesh):
    return jax.shard_map(
        per_device,
        mesh=mesh,
        in_specs=(
            P(("img", "txt"), None),
            P(("img", "txt"), None),
            P(("img", "txt")),
            P(),
            P(),
            P(("img", "txt"), None),
        ),
        out_specs=(P(("img", "txt"), None), P(("img", "txt"), None), P()),
        check_vma=False,
    )
```

```python
import functools

import jax
import jax.numpy as jnp
from jax import lax
from jax.experimental import pallas as pl
from jax.experimental.pallas import tpu as pltpu
from jax.sharding import PartitionSpec as P

ROWS = 384
BLK = 4
SIDE = 4
HALF = BLK // 2
EPS = 1e-06
VMEM = 60 * 1024 * 1024
CHUNK = 48

FAR = 2
EARLY = ((0, 1), (0, 3), (FAR, 0), (FAR, 1), (FAR, 3))
OPPOSITE = ((FAR, FAR), (0, FAR), (1, FAR), (3, FAR))
LATE = tuple((i, j) for i in (1, 3) for j in (0, 1, 3))
GROUPS = (EARLY, OPPOSITE, LATE)
COEF_AT = {slot: (source, known.index(slot)) for source, known in enumerate(GROUPS) for slot in known}
POSITIVE = "positive"
SLOT_NUMBERS = 3 * SIDE * SIDE
NOTES = 16
ANY = pl.BlockSpec(memory_space=pl.ANY)
SMEM = pl.BlockSpec(memory_space=pltpu.SMEM)
WHOLE = pl.BlockSpec(memory_space=pltpu.VMEM)


def params():
    return dict(
        compiler_params=pltpu.CompilerParams(vmem_limit_bytes=VMEM),
        cost_estimate=pl.CostEstimate(flops=1000, bytes_accessed=1000, transcendentals=0),
    )


def pipelined(items, ahead):
    for start, _, _ in items[:ahead]:
        start()
    for at, (_, wait, work) in enumerate(items):
        wait()
        if at + ahead < len(items):
            items[at + ahead][0]()
        work()


def chunked(chunks, sources, targets, work):
    def item(c):
        def start():
            for copy in sources[c]:
                copy.start()

        def wait():
            for copy in sources[c]:
                copy.wait()

        def run():
            work(c)
            targets[c].start()

        return start, wait, run

    pipelined([item(c) for c in range(chunks)], chunks)
    for copy in targets:
        copy.wait()


def normalize_kernel(chunks, images, texts, notes, xa, xb, ya, yb, held, done, sems, note_sems):
    half = images.shape[0] // 2
    step = 2 * half // chunks
    note_copies = [
        pltpu.make_async_copy(notes, out.at[pl.ds(half, NOTES)], note_sems.at[k]) for k, out in enumerate((xa, xb))]
    for copy in note_copies:
        copy.start()
    sources, targets = [], []
    for c in range(2 * chunks):
        emb, outs = ((images, (xa, xb)), (texts, (ya, yb)))[c // chunks]
        at = c % chunks * step
        sources.append([pltpu.make_async_copy(emb.at[pl.ds(at, step)], held.at[c], sems.at[0, c])])
        out = outs[at // half].at[pl.ds(at % half, step)]
        targets.append(pltpu.make_async_copy(done.at[c], out, sems.at[1, c]))

    def work(c):
        values = held[c].astype(jnp.float32)
        inverse = lax.rsqrt(jnp.sum(values * values, axis=-1, keepdims=True) + EPS)
        done[c] = (values * inverse).astype(jnp.bfloat16)

    chunked(2 * chunks, sources, targets, work)
    for copy in note_copies:
        copy.wait()


def normalize(images, texts, notes):
    rows, width = images.shape
    chunks = 4
    held = pltpu.VMEM((2 * chunks, rows // chunks, width), jnp.bfloat16)
    half = jax.ShapeDtypeStruct((rows // 2, width), jnp.bfloat16)
    noted = jax.ShapeDtypeStruct((rows // 2 + NOTES, width), jnp.bfloat16)
    return pl.pallas_call(
        functools.partial(normalize_kernel, chunks),
        in_specs=[ANY] * 3,
        out_specs=[ANY] * 4,
        out_shape=[noted, noted, half, half],
        scratch_shapes=[held, held, pltpu.SemaphoreType.DMA((2, 2 * chunks)), pltpu.SemaphoreType.DMA((2,))],
        **params(),
    )(images, texts, notes)


def when(condition, work):
    if condition is True:
        work()
    else:
        pl.when(condition)(work)


def block_copies(refs, offset, index, dst, sem):
    copies = []
    for part in range(2):
        if isinstance(index, int):
            local, inside = index % HALF, index // HALF == part
        else:
            local = jnp.clip(index - part * HALF, 0, HALF - 1)
            inside = (index >= part * HALF) & (index < (part + 1) * HALF)
        rows = pl.ds(local * ROWS if isinstance(index, int) else pl.multiple_of(local * ROWS, ROWS), ROWS)
        if inside is not False:
            copies.append((inside, pltpu.make_async_copy(refs[offset][part].at[rows], dst, sem)))
    return copies


def start_copies(live, copies):
    for inside, copy in copies:
        if inside is True or live is True:
            when(live if inside is True else inside, copy.start)
        else:
            when(live & inside, copy.start)


def split_refs(refs):
    return {offset: refs[2 * offset:2 * offset + 2] for offset in range(SIDE)}


N_REFS = 2 * SIDE


def columns(row):
    return jnp.transpose(jnp.broadcast_to(row, (128, ROWS)))


def coefficients(sims_ref, coef_ref, weight_ref, scale, offset, positive):
    def step(at, sums):
        loss_sum, coef_sum, dot_sum = sums
        rows = pl.ds(pl.multiple_of(at * CHUNK, CHUNK), CHUNK)
        sims = sims_ref[rows, :]
        logits = scale * sims + offset
        weight = jnp.concatenate([weight_ref[rows, :]] * (ROWS // 128), axis=1)
        scaled_weight = weight * scale
        if positive:
            row = lax.broadcasted_iota(jnp.int32, sims.shape, 0) + at * CHUNK
            col = lax.broadcasted_iota(jnp.int32, sims.shape, 1)
            diagonal = row == col
            logits = jnp.where(diagonal, -logits, logits)
            scaled_weight = jnp.where(diagonal, -scaled_weight, scaled_weight)
        power = jnp.exp(logits)
        one_more = 1.0 + power
        coef = scaled_weight * (power / one_more)
        loss = weight * jnp.log(one_more)
        coef_ref[rows, :] = coef.astype(jnp.bfloat16)

        def fold(value):
            return jnp.sum(value.reshape(CHUNK // 8, 8, ROWS), axis=0)

        return (loss_sum + fold(loss), coef_sum + fold(coef), dot_sum + fold(coef * sims))

    zero = jnp.zeros((8, ROWS), jnp.float32)
    return lax.fori_loop(0, ROWS // CHUNK, step, (zero, zero, zero), unroll=True)


def dot(lhs, rhs, dims):
    return lax.dot_general(lhs, rhs, (dims, ((), ())), preferred_element_type=jnp.float32)


NT = ((1,), (1,))
NN = ((1,), (0,))
TN = ((0,), (0,))


def read_entry(plans, place, slot):
    if slot[0] == POSITIVE:
        return slot[1], slot[1], True
    owner = (place[0] + slot[1]) % SIDE * SIDE + place[1]
    at = slot[0] * SLOT_NUMBERS + owner * 3
    return plans[at], plans[at + 1], plans[at + 2] > 0


def offsets_of(slot):
    return (0, 0) if slot[0] == POSITIVE else slot


def block_item(live, wanted, dst, sem, extra_copies, work):
    def start():
        for k, (refs, offset, index) in enumerate(wanted):
            start_copies(live, block_copies(refs, offset, index, dst[k], sem[k]))
        start_copies(live, [(True, copy) for copy in extra_copies])

    def wait():
        def waits():
            for k, (refs, offset, index) in enumerate(wanted):
                pltpu.make_async_copy(refs[0][0].at[pl.ds(0, ROWS)], dst[k], sem[k]).wait()
            for copy in extra_copies:
                copy.wait()

        when(live, waits)

    return start, wait, lambda: when(live, work)


def add_tile(acc, seen, index, tile):
    acc[index] = jnp.where(seen[index] > 0, acc[index], 0.0) + tile
    seen[index] = 1


def send_sums(acc, seen, staged, outs, sems, arrived=None):
    copies = []
    for b in range(BLK):
        total = jnp.where(seen[b] > 0, acc[b], 0.0)
        if arrived is not None:
            total = total + arrived[b].astype(jnp.float32)
        staged[b] = total.astype(staged.dtype)
        rows = pl.ds(b % HALF * ROWS, ROWS)
        copies.append(pltpu.make_async_copy(staged.at[b], outs[b // HALF].at[rows], sems.at[b]))
        copies[-1].start()
    return copies


def arrivals_of(parts, buf, sems):
    return [
        pltpu.make_async_copy(parts[b // HALF].at[pl.ds(b % HALF * ROWS, ROWS)], buf.at[b], sems.at[b])
        for b in range(BLK)]


def pairs_kernel(slots, sides, n_arrived, *refs):
    plans, place, scalars, image_rows = refs[0:4]
    at = 4
    xrefs, yrefs = split_refs(refs[at:at + N_REFS]), split_refs(refs[at + N_REFS:at + 2 * N_REFS])
    at += 2 * N_REFS
    arrived = refs[at:at + n_arrived]
    at += n_arrived
    coef_out, stats_out = refs[at], refs[at + 1]
    at += 2
    outs = refs[at:at + 2 * len(sides)]
    at += len(outs)
    xbuf, ybuf, wbuf, sims, coefs, sems, acc, seen, staged, osems = refs[at:at + 10]
    arrivals = arrivals_of(arrived, *refs[-2:]) if n_arrived else []
    scale, offset = scalars[0], scalars[1]
    copies = []

    def slot_item(s, slot):
        (i, j), (p, q, live) = offsets_of(slot), read_entry(plans, place, slot)

        def work():
            wbuf[...] = columns(image_rows[pl.ds(i * BLK + p, 1), :])
            for part in range(2):
                rows = pl.ds(part * (ROWS // 2), ROWS // 2)
                sims[rows, :] = dot(xbuf[s, rows, :], ybuf[s], NT)
            sums = coefficients(sims, coefs.at[s], wbuf, scale, offset, slot[0] == POSITIVE)
            for k in range(3):
                stats_out[k] += sums[k]
            pltpu.make_async_copy(coefs.at[s], coef_out.at[s], sems.at[2, s]).start()
            if "x" in sides and i == FAR:
                add_tile(acc.at[0], seen.at[0], p, dot(coefs[s], ybuf[s], NN))
            if "y" in sides and j == FAR:
                add_tile(acc.at[1], seen.at[1], q, dot(coefs[s], xbuf[s], TN))

        wanted = ((xrefs, i, p), (yrefs, j, q))
        return block_item(live, wanted, (xbuf.at[s], ybuf.at[s]), (sems.at[0, s], sems.at[1, s]), (), work)

    def send(side):
        for arrival in arrivals if side == 0 else ():
            arrival.wait()
        copies.extend(send_sums(
            acc.at[side], seen.at[side], staged.at[side], outs[2 * side:2 * side + 2], osems.at[side],
            refs[-2] if arrivals and side == 0 else None))

    stats_out[...] = jnp.zeros_like(stats_out)
    for side in range(len(sides)):
        for b in range(BLK):
            seen[side, b] = 0
    items = [slot_item(s, slot) for s, slot in enumerate(slots)]
    last = {"x": max([s for s, slot in enumerate(slots) if slot[0] == FAR], default=0), "y": len(slots) - 1}
    for side in reversed(range(len(sides))):
        at = last[sides[side]] + 1
        items.insert(at, (lambda: None, lambda: None, functools.partial(send, side)))
    items.insert(1, (lambda: [arrival.start() for arrival in arrivals], lambda: None, lambda: None))
    pipelined(items, 3)
    for s, slot in enumerate(slots):
        live = read_entry(plans, place, slot)[2]
        when(live, pltpu.make_async_copy(coefs.at[s], coef_out.at[s], sems.at[2, s]).wait)
    for copy in copies:
        copy.wait()


def pairs(slots, sides, arrived, small, images, texts):
    width = texts[0].shape[1]
    total = len(slots)
    held = max(len(sides), 1)
    blocks = (held, BLK, ROWS, width) if sides else (1, 1, 8, 128)
    out_shape = [
        jax.ShapeDtypeStruct((total, ROWS, ROWS), jnp.bfloat16),
        jax.ShapeDtypeStruct((3, 8, ROWS), jnp.float32),
    ] + [jax.ShapeDtypeStruct((HALF * ROWS, width), jnp.bfloat16)] * (2 * len(sides))
    scratch = [
        pltpu.VMEM((total, ROWS, width), jnp.bfloat16),
        pltpu.VMEM((total, ROWS, width), jnp.bfloat16),
        pltpu.VMEM((ROWS, 128), jnp.float32),
        pltpu.VMEM((ROWS, ROWS), jnp.float32),
        pltpu.VMEM((total, ROWS, ROWS), jnp.bfloat16),
        pltpu.SemaphoreType.DMA((3, total)),
        pltpu.VMEM(blocks, jnp.float32),
        pltpu.SMEM((held, BLK), jnp.int32),
        pltpu.VMEM(blocks, jnp.bfloat16),
        pltpu.SemaphoreType.DMA((held, BLK)),
    ]
    if arrived:
        scratch += [pltpu.VMEM((BLK, ROWS, width), jnp.bfloat16), pltpu.SemaphoreType.DMA((BLK,))]
    return pl.pallas_call(
        functools.partial(pairs_kernel, slots, sides, len(arrived)),
        in_specs=[SMEM, SMEM, SMEM, WHOLE] + [ANY] * (2 * N_REFS + len(arrived)),
        out_specs=[ANY, WHOLE] + [ANY] * (len(out_shape) - 2),
        out_shape=out_shape,
        scratch_shapes=scratch,
        **params(),
    )(*small, *images, *texts, *arrived)


def grads_kernel(axis, groups, n_arrived, *refs):
    plans, place = refs[0:2]
    other = split_refs(refs[2:2 + N_REFS])
    at = 2 + N_REFS
    coefs = refs[at:at + len(GROUPS)]
    arrived = refs[at + len(GROUPS):at + len(GROUPS) + n_arrived]
    at += len(GROUPS) + n_arrived
    outs = refs[at:at + 2 * len(groups)]
    buf, cbuf, acc, seen, staged, sems, osems = refs[at + 2 * len(groups):at + 2 * len(groups) + 7]
    mine = 0 if axis == "x" else 1
    dims = NN if axis == "x" else TN
    items, copies, arrivals = [], [], []
    if n_arrived:
        abuf, asems = refs[-2:]
        arrivals = arrivals_of(arrived, abuf, asems)

    def slot_item(at, group, last, slot, source, index):
        entry = read_entry(plans, place, slot)
        copy = pltpu.make_async_copy(coefs[source].at[index], cbuf.at[at], sems.at[1, at])

        def work():
            add_tile(acc.at[group], seen.at[group], entry[mine], dot(cbuf[at], buf[at], dims))

        wanted = ((other, offsets_of(slot)[1 - mine], entry[1 - mine]),)
        start, wait, run = block_item(entry[2], wanted, (buf.at[at],), (sems.at[0, at],), (copy,), work)

        def run_and_send():
            run()
            if last:
                for arrival in arrivals:
                    arrival.wait()
                copies.extend(send_sums(
                    acc.at[group], seen.at[group], staged.at[group], outs[2 * group:2 * group + 2], osems.at[group],
                    abuf if n_arrived else None))

        return start, wait, run_and_send

    for group, entries in enumerate(groups):
        for b in range(BLK):
            seen[group, b] = 0
        for entry in entries:
            items.append(slot_item(len(items), group, entry is entries[-1], *entry))
    for arrival in arrivals:
        arrival.start()
    pipelined(items, 5)
    for copy in copies:
        copy.wait()


def grads(axis, offsets, with_positive, small, blocks, coefs, arrived=()):
    width = blocks[0].shape[1]
    groups = []
    for offset in offsets:
        group = []
        for neighbour in (0, 1, 3, 2):
            slot = (offset, neighbour) if axis == "x" else (neighbour, offset)
            if slot != (0, 0):
                group.append((slot, *COEF_AT[slot]))
        if with_positive:
            group += [((POSITIVE, b), 0, len(EARLY) + b) for b in range(BLK)]
        groups.append(tuple(group))
    total = sum(len(group) for group in groups)
    scratch = [
        pltpu.VMEM((total, ROWS, width), jnp.bfloat16),
        pltpu.VMEM((total, ROWS, ROWS), jnp.bfloat16),
        pltpu.VMEM((len(groups), BLK, ROWS, width), jnp.float32),
        pltpu.SMEM((len(groups), BLK), jnp.int32),
        pltpu.VMEM((len(groups), BLK, ROWS, width), jnp.bfloat16),
        pltpu.SemaphoreType.DMA((2, total)),
        pltpu.SemaphoreType.DMA((len(groups), BLK)),
    ]
    if arrived:
        scratch += [pltpu.VMEM((BLK, ROWS, width), jnp.bfloat16), pltpu.SemaphoreType.DMA((BLK,))]
    return pl.pallas_call(
        functools.partial(grads_kernel, axis, tuple(groups), len(arrived)),
        in_specs=[SMEM, SMEM] + [ANY] * (N_REFS + len(GROUPS) + len(arrived)),
        out_specs=[ANY] * (2 * len(groups)),
        out_shape=[jax.ShapeDtypeStruct((HALF * ROWS, width), jnp.bfloat16)] * (2 * len(groups)),
        scratch_shapes=scratch,
        **params(),
    )(*small[:2], *blocks, *coefs, *arrived)


def finish_kernel(chunks, emb, own_a, own_b, last_a, last_b, out, embs, owns, lasts, done, sems):
    half = own_a.shape[0]
    step = 2 * half // chunks
    sources, targets = [], []
    for c in range(chunks):
        own, last = ((own_a, last_a), (own_b, last_b))[c * step // half]
        rows, of_whole = pl.ds(c * step % half, step), pl.ds(c * step, step)
        pieces = ((emb, of_whole, embs), (own, rows, owns), (last, rows, lasts))
        sources.append([
            pltpu.make_async_copy(ref.at[at], held.at[c], sems.at[k, c]) for k, (ref, at, held) in enumerate(pieces)])
        targets.append(pltpu.make_async_copy(done.at[c], out.at[of_whole], sems.at[3, c]))

    def work(c):
        values = embs[c].astype(jnp.float32)
        inverse = lax.rsqrt(jnp.sum(values * values, axis=-1, keepdims=True) + EPS)
        total = owns[c].astype(jnp.float32) + lasts[c].astype(jnp.float32)
        inner = jnp.sum(values * total, axis=-1, keepdims=True) * (inverse * inverse)
        done[c] = (inverse * (total - values * inner)).astype(jnp.bfloat16)

    chunked(chunks, sources, targets, work)


def finish(emb, own, last):
    rows, width = emb.shape
    chunks = 8
    held = pltpu.VMEM((chunks, rows // chunks, width), jnp.bfloat16)
    return pl.pallas_call(
        functools.partial(finish_kernel, chunks),
        in_specs=[ANY] * 5,
        out_specs=ANY,
        out_shape=jax.ShapeDtypeStruct(emb.shape, jnp.bfloat16),
        scratch_shapes=[held] * 4 + [pltpu.SemaphoreType.DMA((4, chunks))],
        **params(),
    )(emb, *own, *last)


def shift(value, axis, by):
    pairs_of = []
    for y in range(SIDE):
        for x in range(SIDE):
            to = (y * SIDE + (x + by) % SIDE) if axis == "x" else ((y + by) % SIDE * SIDE + x)
            pairs_of.append((y * SIDE + x, to))
    return lax.ppermute(value, "txt", pairs_of)


def after(values, done):
    out = lax.optimization_barrier(tuple(values) + tuple(done))
    return out[:len(values)]


def both_ways(axis, forward, backward, done=()):
    if done:
        (forward,), (backward,) = after((forward,), done[:1]), after((backward,), done[1:])
    return shift(forward, axis, 1), shift(backward, axis, -1)


def add_partner(value, axis, bit):
    size = lax.axis_size(axis)
    return value + lax.ppermute(value, axis, [(i, i ^ bit) for i in range(size)])


def join_kernel(chunks, ours_a, arrived_a, ours_b, arrived_b, out_a, out_b, ours, arrived, done, sems):
    step = 2 * ours_a.shape[0] // chunks
    sources, targets = [], []
    for c in range(chunks):
        mine, other, out = ((ours_a, arrived_a, out_a), (ours_b, arrived_b, out_b))[2 * c // chunks]
        rows = pl.ds(c * step % ours_a.shape[0], step)
        sources.append([
            pltpu.make_async_copy(mine.at[rows], ours.at[c], sems.at[0, c]),
            pltpu.make_async_copy(other.at[rows], arrived.at[c], sems.at[1, c])])
        targets.append(pltpu.make_async_copy(done.at[c], out.at[rows], sems.at[2, c]))

    def work(c):
        done[c] = (ours[c].astype(jnp.float32) + arrived[c].astype(jnp.float32)).astype(jnp.bfloat16)

    chunked(chunks, sources, targets, work)


def join(ours_a, arrived_a, ours_b, arrived_b):
    rows, width = ours_a.shape
    chunks = 4
    held = pltpu.VMEM((chunks, 2 * rows // chunks, width), jnp.bfloat16)
    return pl.pallas_call(
        functools.partial(join_kernel, chunks),
        in_specs=[ANY] * 4,
        out_specs=[ANY] * 2,
        out_shape=[jax.ShapeDtypeStruct(ours_a.shape, jnp.bfloat16)] * 2,
        scratch_shapes=[held] * 3 + [pltpu.SemaphoreType.DMA((3, chunks))],
        **params(),
    )(ours_a, arrived_a, ours_b, arrived_b)


def per_device(image_emb, text_emb, row_weight, log_scale, bias, pair_slots):
    width = image_emb.shape[1]
    half = HALF * ROWS
    scale = jnp.exp(log_scale[0])
    scalars = jnp.stack([scale, bias[0]])
    weights = jnp.pad(row_weight.reshape(BLK, ROWS), ((0, 0), (0, width - ROWS)))
    plan = jnp.pad(pair_slots.astype(jnp.bfloat16).reshape(1, -1), ((0, NOTES - BLK - 1), (0, width - SLOT_NUMBERS)))
    xa, xb, ya, yb = normalize(image_emb, text_emb, jnp.concatenate([weights, plan]))

    x1 = both_ways("x", xa, xb)
    y1 = both_ways("y", ya, yb)
    x2 = both_ways("x", *x1)
    y2 = both_ways("y", yb, ya, y1)
    x3 = both_ways("x", xb, xa, x2)
    y3 = both_ways("y", *y1, y2)
    y_next, y_prev = (y2[1], y1[1]), (y1[0], y2[0])
    own_x, own_y = (xa, xb), (ya, yb)

    notes = [message[half:half + BLK + 1, :ROWS].astype(jnp.float32) for message in (xa, x1[1], x2[0], x1[0])]
    weight_rows = jnp.concatenate([note[:BLK] for note in notes])
    plans = jnp.concatenate([note[BLK, :SLOT_NUMBERS] for note in notes]).astype(jnp.int32)
    me = lax.axis_index("txt")
    place = jnp.stack([me // SIDE, me % SIDE]).astype(jnp.int32)
    small = (plans, place, scalars, weight_rows)

    early_x = (*own_x, *own_x, *x2, *own_x)
    early_y = (*own_y, *y_next, *own_y, *y_prev)
    positives = tuple((POSITIVE, b) for b in range(BLK))
    early, early_stats, *dx_far = pairs(EARLY + positives, ("x",), (), small, early_x, early_y)
    early, early_stats, *arrived = lax.optimization_barrier((early, early_stats, *x3, *y3))
    x3, y3 = arrived[:2], arrived[2:]
    x_next, x_prev = (x3[1], x1[1]), (x1[0], x3[0])
    images = (*own_x, *x_next, *x2, *x_prev)
    texts = (*own_y, *y_next, *y3, *y_prev)

    opposite, opposite_stats, *far = pairs(OPPOSITE, ("x", "y"), tuple(dx_far), small, images, texts)
    x4 = both_ways("x", *far[:2])
    y4 = both_ways("y", *far[2:])
    late, late_stats = pairs(LATE, (), (), after(small, far), images, texts)
    coefs = (early, opposite, late)
    dx_next_a, dx_next_b, dx_prev_a, dx_prev_b = grads("x", (1, 3), False, small, texts, coefs)
    dy_next_a, dy_next_b, dy_prev_a, dy_prev_b = grads("y", (1, 3), False, small, images, coefs)

    sums = jnp.sum((early_stats + opposite_stats + late_stats).reshape(3, -1), axis=1)
    stats = jnp.stack([sums[0], sums[2], sums[1] / scale])
    stats = add_partner(stats, "txt", 1)
    *x4, stats = lax.optimization_barrier((*x4, stats))
    x5 = both_ways("x", dx_next_b, dx_prev_a, x4)
    y5 = both_ways("y", dy_next_b, dy_prev_a, y4)
    joined_x = join(dx_next_a, x4[0], dx_prev_b, x4[1])
    joined_y = join(dy_next_a, y4[0], dy_prev_b, y4[1])
    for bit in (1, 2, 4):
        stats = add_partner(stats, "img", bit)
    stats = add_partner(stats, "txt", SIDE)
    *y5, stats = lax.optimization_barrier((*y5, stats))
    x6 = both_ways("x", *joined_x, x5)
    y6 = both_ways("y", *joined_y, y5)
    own_small = after(small, (*x5, *y5))
    dx_own = grads("x", (0,), True, own_small, texts, coefs, (x5[1], x5[0]))
    dy_own = grads("y", (0,), True, own_small, images, coefs, (y5[1], y5[0]))
    stats = add_partner(stats, "txt", 2 * SIDE)
    y6 = after(y6, (*dx_own, *dy_own))
    grad_text = finish(text_emb, dy_own, y6)
    *x6, stats = lax.optimization_barrier((*x6, stats, grad_text))[:3]
    wide = add_partner(jnp.broadcast_to(stats[:, None], (3, 1152)), "txt", 2)
    stats = wide[:, 0]
    grad_image = finish(image_emb, dx_own, x6)
    count = BLK * ROWS * lax.axis_size("img") * lax.axis_size("txt")
    return (grad_image, grad_text, stats / count)


def solution(mesh):
    return jax.shard_map(
        per_device,
        mesh=mesh,
        in_specs=(
            P(("img", "txt"), None),
            P(("img", "txt"), None),
            P(("img", "txt")),
            P(),
            P(),
            P(("img", "txt"), None),
        ),
        out_specs=(P(("img", "txt"), None), P(("img", "txt"), None), P()),
        check_vma=False,
    )
```

```python
import functools

import jax
import jax.numpy as jnp
from jax import lax
from jax.experimental import pallas as pl
from jax.experimental.pallas import tpu as pltpu
from jax.sharding import PartitionSpec as P

ROWS = 384
BLK = 4
SIDE = 4
HALF = BLK // 2
EPS = 1e-06
VMEM = 60 * 1024 * 1024
CHUNK = 48

FAR = 2
EARLY = ((0, 1), (0, 3), (FAR, 0), (FAR, 1), (FAR, 3))
OPPOSITE = ((FAR, FAR), (0, FAR), (1, FAR), (3, FAR))
LATE = tuple((i, j) for i in (1, 3) for j in (0, 1, 3))
GROUPS = (EARLY, OPPOSITE, LATE)
COEF_AT = {slot: (source, known.index(slot)) for source, known in enumerate(GROUPS) for slot in known}
POSITIVE = "positive"
SLOT_NUMBERS = 3 * SIDE * SIDE
NOTES = 16
ANY = pl.BlockSpec(memory_space=pl.ANY)
SMEM = pl.BlockSpec(memory_space=pltpu.SMEM)
WHOLE = pl.BlockSpec(memory_space=pltpu.VMEM)


def params():
    return dict(
        compiler_params=pltpu.CompilerParams(vmem_limit_bytes=VMEM),
        cost_estimate=pl.CostEstimate(flops=1000, bytes_accessed=1000, transcendentals=0),
    )


def pipelined(items, ahead):
    for start, _, _ in items[:ahead]:
        start()
    for at, (_, wait, work) in enumerate(items):
        wait()
        if at + ahead < len(items):
            items[at + ahead][0]()
        work()


def chunked(chunks, sources, targets, work):
    def item(c):
        def start():
            for copy in sources[c]:
                copy.start()

        def wait():
            for copy in sources[c]:
                copy.wait()

        def run():
            work(c)
            targets[c].start()

        return start, wait, run

    pipelined([item(c) for c in range(chunks)], chunks)
    for copy in targets:
        copy.wait()


def normalize_kernel(chunks, images, texts, notes, xa, xb, ya, yb, held, done, sems, note_sems):
    half = images.shape[0] // 2
    step = 2 * half // chunks
    note_copies = [
        pltpu.make_async_copy(notes, out.at[pl.ds(half, NOTES)], note_sems.at[k]) for k, out in enumerate((xa, xb))]
    for copy in note_copies:
        copy.start()
    sources, targets = [], []
    for c in range(2 * chunks):
        emb, outs = ((images, (xa, xb)), (texts, (ya, yb)))[c // chunks]
        at = c % chunks * step
        sources.append([pltpu.make_async_copy(emb.at[pl.ds(at, step)], held.at[c], sems.at[0, c])])
        out = outs[at // half].at[pl.ds(at % half, step)]
        targets.append(pltpu.make_async_copy(done.at[c], out, sems.at[1, c]))

    def work(c):
        values = held[c].astype(jnp.float32)
        inverse = lax.rsqrt(jnp.sum(values * values, axis=-1, keepdims=True) + EPS)
        done[c] = (values * inverse).astype(jnp.bfloat16)

    chunked(2 * chunks, sources, targets, work)
    for copy in note_copies:
        copy.wait()


def normalize(images, texts, notes):
    rows, width = images.shape
    chunks = 4
    held = pltpu.VMEM((2 * chunks, rows // chunks, width), jnp.bfloat16)
    half = jax.ShapeDtypeStruct((rows // 2, width), jnp.bfloat16)
    noted = jax.ShapeDtypeStruct((rows // 2 + NOTES, width), jnp.bfloat16)
    return pl.pallas_call(
        functools.partial(normalize_kernel, chunks),
        in_specs=[ANY] * 3,
        out_specs=[ANY] * 4,
        out_shape=[noted, noted, half, half],
        scratch_shapes=[held, held, pltpu.SemaphoreType.DMA((2, 2 * chunks)), pltpu.SemaphoreType.DMA((2,))],
        **params(),
    )(images, texts, notes)


def when(condition, work):
    if condition is True:
        work()
    else:
        pl.when(condition)(work)


def block_copies(refs, offset, index, dst, sem):
    copies = []
    for part in range(2):
        if isinstance(index, int):
            local, inside = index % HALF, index // HALF == part
        else:
            local = jnp.clip(index - part * HALF, 0, HALF - 1)
            inside = (index >= part * HALF) & (index < (part + 1) * HALF)
        rows = pl.ds(local * ROWS if isinstance(index, int) else pl.multiple_of(local * ROWS, ROWS), ROWS)
        if inside is not False:
            copies.append((inside, pltpu.make_async_copy(refs[offset][part].at[rows], dst, sem)))
    return copies


def start_copies(live, copies):
    for inside, copy in copies:
        if inside is True or live is True:
            when(live if inside is True else inside, copy.start)
        else:
            when(live & inside, copy.start)


def split_refs(refs):
    return {offset: refs[2 * offset:2 * offset + 2] for offset in range(SIDE)}


N_REFS = 2 * SIDE


def columns(row):
    return jnp.transpose(jnp.broadcast_to(row, (128, ROWS)))


def coefficients(sims_ref, coef_ref, weight_ref, scale, offset, positive):
    def step(at, sums):
        loss_sum, coef_sum, dot_sum = sums
        rows = pl.ds(pl.multiple_of(at * CHUNK, CHUNK), CHUNK)
        sims = sims_ref[rows, :]
        logits = scale * sims + offset
        weight = jnp.concatenate([weight_ref[rows, :]] * (ROWS // 128), axis=1)
        scaled_weight = weight * scale
        if positive:
            row = lax.broadcasted_iota(jnp.int32, sims.shape, 0) + at * CHUNK
            col = lax.broadcasted_iota(jnp.int32, sims.shape, 1)
            diagonal = row == col
            logits = jnp.where(diagonal, -logits, logits)
            scaled_weight = jnp.where(diagonal, -scaled_weight, scaled_weight)
        power = jnp.exp(logits)
        one_more = 1.0 + power
        coef = scaled_weight * (power / one_more)
        loss = weight * jnp.log(one_more)
        coef_ref[rows, :] = coef.astype(jnp.bfloat16)

        def fold(value):
            return jnp.sum(value.reshape(CHUNK // 8, 8, ROWS), axis=0)

        return (loss_sum + fold(loss), coef_sum + fold(coef), dot_sum + fold(coef * sims))

    zero = jnp.zeros((8, ROWS), jnp.float32)
    return lax.fori_loop(0, ROWS // CHUNK, step, (zero, zero, zero), unroll=True)


def dot(lhs, rhs, dims):
    return lax.dot_general(lhs, rhs, (dims, ((), ())), preferred_element_type=jnp.float32)


NT = ((1,), (1,))
NN = ((1,), (0,))
TN = ((0,), (0,))


def read_entry(plans, place, slot):
    if slot[0] == POSITIVE:
        return slot[1], slot[1], True
    owner = (place[0] + slot[1]) % SIDE * SIDE + place[1]
    at = slot[0] * SLOT_NUMBERS + owner * 3
    return plans[at], plans[at + 1], plans[at + 2] > 0


def offsets_of(slot):
    return (0, 0) if slot[0] == POSITIVE else slot


def block_item(live, wanted, dst, sem, extra_copies, work):
    def start():
        for k, (refs, offset, index) in enumerate(wanted):
            start_copies(live, block_copies(refs, offset, index, dst[k], sem[k]))
        start_copies(live, [(True, copy) for copy in extra_copies])

    def wait():
        def waits():
            for k, (refs, offset, index) in enumerate(wanted):
                pltpu.make_async_copy(refs[0][0].at[pl.ds(0, ROWS)], dst[k], sem[k]).wait()
            for copy in extra_copies:
                copy.wait()

        when(live, waits)

    return start, wait, lambda: when(live, work)


def add_tile(acc, seen, index, tile):
    acc[index] = jnp.where(seen[index] > 0, acc[index], 0.0) + tile
    seen[index] = 1


def send_sums(acc, seen, staged, outs, sems, arrived=None):
    copies = []
    for b in range(BLK):
        total = jnp.where(seen[b] > 0, acc[b], 0.0)
        if arrived is not None:
            total = total + arrived[b].astype(jnp.float32)
        staged[b] = total.astype(staged.dtype)
        rows = pl.ds(b % HALF * ROWS, ROWS)
        copies.append(pltpu.make_async_copy(staged.at[b], outs[b // HALF].at[rows], sems.at[b]))
        copies[-1].start()
    return copies


def arrivals_of(parts, buf, sems):
    return [
        pltpu.make_async_copy(parts[b // HALF].at[pl.ds(b % HALF * ROWS, ROWS)], buf.at[b], sems.at[b])
        for b in range(BLK)]


def pairs_kernel(slots, sides, n_arrived, *refs):
    plans, place, scalars, image_rows = refs[0:4]
    at = 4
    xrefs, yrefs = split_refs(refs[at:at + N_REFS]), split_refs(refs[at + N_REFS:at + 2 * N_REFS])
    at += 2 * N_REFS
    arrived = refs[at:at + n_arrived]
    at += n_arrived
    coef_out, stats_out = refs[at], refs[at + 1]
    at += 2
    outs = refs[at:at + 2 * len(sides)]
    at += len(outs)
    xbuf, ybuf, wbuf, sims, coefs, sems, acc, seen, staged, osems = refs[at:at + 10]
    arrivals = arrivals_of(arrived, *refs[-2:]) if n_arrived else []
    scale, offset = scalars[0], scalars[1]
    copies = []

    def slot_item(s, slot):
        (i, j), (p, q, live) = offsets_of(slot), read_entry(plans, place, slot)

        def work():
            wbuf[...] = columns(image_rows[pl.ds(i * BLK + p, 1), :])
            for part in range(2):
                rows = pl.ds(part * (ROWS // 2), ROWS // 2)
                sims[rows, :] = dot(xbuf[s, rows, :], ybuf[s], NT)
            sums = coefficients(sims, coefs.at[s], wbuf, scale, offset, slot[0] == POSITIVE)
            for k in range(3):
                stats_out[k] += sums[k]
            pltpu.make_async_copy(coefs.at[s], coef_out.at[s], sems.at[2, s]).start()
            if "x" in sides and i == FAR:
                add_tile(acc.at[0], seen.at[0], p, dot(coefs[s], ybuf[s], NN))
            if "y" in sides and j == FAR:
                add_tile(acc.at[1], seen.at[1], q, dot(coefs[s], xbuf[s], TN))

        wanted = ((xrefs, i, p), (yrefs, j, q))
        return block_item(live, wanted, (xbuf.at[s], ybuf.at[s]), (sems.at[0, s], sems.at[1, s]), (), work)

    def send(side):
        for arrival in arrivals if side == 0 else ():
            arrival.wait()
        copies.extend(send_sums(
            acc.at[side], seen.at[side], staged.at[side], outs[2 * side:2 * side + 2], osems.at[side],
            refs[-2] if arrivals and side == 0 else None))

    stats_out[...] = jnp.zeros_like(stats_out)
    for side in range(len(sides)):
        for b in range(BLK):
            seen[side, b] = 0
    items = [slot_item(s, slot) for s, slot in enumerate(slots)]
    last = {"x": max([s for s, slot in enumerate(slots) if slot[0] == FAR], default=0), "y": len(slots) - 1}
    for side in reversed(range(len(sides))):
        at = last[sides[side]] + 1
        items.insert(at, (lambda: None, lambda: None, functools.partial(send, side)))
    items.insert(1, (lambda: [arrival.start() for arrival in arrivals], lambda: None, lambda: None))
    pipelined(items, 6)
    for s, slot in enumerate(slots):
        live = read_entry(plans, place, slot)[2]
        when(live, pltpu.make_async_copy(coefs.at[s], coef_out.at[s], sems.at[2, s]).wait)
    for copy in copies:
        copy.wait()


def pairs(slots, sides, arrived, small, images, texts):
    width = texts[0].shape[1]
    total = len(slots)
    held = max(len(sides), 1)
    blocks = (held, BLK, ROWS, width) if sides else (1, 1, 8, 128)
    out_shape = [
        jax.ShapeDtypeStruct((total, ROWS, ROWS), jnp.bfloat16),
        jax.ShapeDtypeStruct((3, 8, ROWS), jnp.float32),
    ] + [jax.ShapeDtypeStruct((HALF * ROWS, width), jnp.bfloat16)] * (2 * len(sides))
    scratch = [
        pltpu.VMEM((total, ROWS, width), jnp.bfloat16),
        pltpu.VMEM((total, ROWS, width), jnp.bfloat16),
        pltpu.VMEM((ROWS, 128), jnp.float32),
        pltpu.VMEM((ROWS, ROWS), jnp.float32),
        pltpu.VMEM((total, ROWS, ROWS), jnp.bfloat16),
        pltpu.SemaphoreType.DMA((3, total)),
        pltpu.VMEM(blocks, jnp.float32),
        pltpu.SMEM((held, BLK), jnp.int32),
        pltpu.VMEM(blocks, jnp.bfloat16),
        pltpu.SemaphoreType.DMA((held, BLK)),
    ]
    if arrived:
        scratch += [pltpu.VMEM((BLK, ROWS, width), jnp.bfloat16), pltpu.SemaphoreType.DMA((BLK,))]
    return pl.pallas_call(
        functools.partial(pairs_kernel, slots, sides, len(arrived)),
        in_specs=[SMEM, SMEM, SMEM, WHOLE] + [ANY] * (2 * N_REFS + len(arrived)),
        out_specs=[ANY, WHOLE] + [ANY] * (len(out_shape) - 2),
        out_shape=out_shape,
        scratch_shapes=scratch,
        **params(),
    )(*small, *images, *texts, *arrived)


def grads_kernel(axis, groups, n_arrived, *refs):
    plans, place = refs[0:2]
    other = split_refs(refs[2:2 + N_REFS])
    at = 2 + N_REFS
    coefs = refs[at:at + len(GROUPS)]
    arrived = refs[at + len(GROUPS):at + len(GROUPS) + n_arrived]
    at += len(GROUPS) + n_arrived
    outs = refs[at:at + 2 * len(groups)]
    buf, cbuf, acc, seen, staged, sems, osems = refs[at + 2 * len(groups):at + 2 * len(groups) + 7]
    mine = 0 if axis == "x" else 1
    dims = NN if axis == "x" else TN
    items, copies, arrivals = [], [], []
    if n_arrived:
        abuf, asems = refs[-2:]
        arrivals = arrivals_of(arrived, abuf, asems)

    def slot_item(at, group, last, slot, source, index):
        entry = read_entry(plans, place, slot)
        copy = pltpu.make_async_copy(coefs[source].at[index], cbuf.at[at], sems.at[1, at])

        def work():
            add_tile(acc.at[group], seen.at[group], entry[mine], dot(cbuf[at], buf[at], dims))

        wanted = ((other, offsets_of(slot)[1 - mine], entry[1 - mine]),)
        start, wait, run = block_item(entry[2], wanted, (buf.at[at],), (sems.at[0, at],), (copy,), work)

        def run_and_send():
            run()
            if last:
                for arrival in arrivals:
                    arrival.wait()
                copies.extend(send_sums(
                    acc.at[group], seen.at[group], staged.at[group], outs[2 * group:2 * group + 2], osems.at[group],
                    abuf if n_arrived else None))

        return start, wait, run_and_send

    for group, entries in enumerate(groups):
        for b in range(BLK):
            seen[group, b] = 0
        for entry in entries:
            items.append(slot_item(len(items), group, entry is entries[-1], *entry))
    for arrival in arrivals:
        arrival.start()
    pipelined(items, 5)
    for copy in copies:
        copy.wait()


def grads(axis, offsets, with_positive, small, blocks, coefs, arrived=()):
    width = blocks[0].shape[1]
    groups = []
    for offset in offsets:
        group = []
        for neighbour in (0, 1, 3, 2):
            slot = (offset, neighbour) if axis == "x" else (neighbour, offset)
            if slot != (0, 0):
                group.append((slot, *COEF_AT[slot]))
        if with_positive:
            group += [((POSITIVE, b), 0, len(EARLY) + b) for b in range(BLK)]
        groups.append(tuple(group))
    total = sum(len(group) for group in groups)
    scratch = [
        pltpu.VMEM((total, ROWS, width), jnp.bfloat16),
        pltpu.VMEM((total, ROWS, ROWS), jnp.bfloat16),
        pltpu.VMEM((len(groups), BLK, ROWS, width), jnp.float32),
        pltpu.SMEM((len(groups), BLK), jnp.int32),
        pltpu.VMEM((len(groups), BLK, ROWS, width), jnp.bfloat16),
        pltpu.SemaphoreType.DMA((2, total)),
        pltpu.SemaphoreType.DMA((len(groups), BLK)),
    ]
    if arrived:
        scratch += [pltpu.VMEM((BLK, ROWS, width), jnp.bfloat16), pltpu.SemaphoreType.DMA((BLK,))]
    return pl.pallas_call(
        functools.partial(grads_kernel, axis, tuple(groups), len(arrived)),
        in_specs=[SMEM, SMEM] + [ANY] * (N_REFS + len(GROUPS) + len(arrived)),
        out_specs=[ANY] * (2 * len(groups)),
        out_shape=[jax.ShapeDtypeStruct((HALF * ROWS, width), jnp.bfloat16)] * (2 * len(groups)),
        scratch_shapes=scratch,
        **params(),
    )(*small[:2], *blocks, *coefs, *arrived)


def finish_kernel(chunks, emb, own_a, own_b, last_a, last_b, out, embs, owns, lasts, done, sems):
    half = own_a.shape[0]
    step = 2 * half // chunks
    sources, targets = [], []
    for c in range(chunks):
        own, last = ((own_a, last_a), (own_b, last_b))[c * step // half]
        rows, of_whole = pl.ds(c * step % half, step), pl.ds(c * step, step)
        pieces = ((emb, of_whole, embs), (own, rows, owns), (last, rows, lasts))
        sources.append([
            pltpu.make_async_copy(ref.at[at], held.at[c], sems.at[k, c]) for k, (ref, at, held) in enumerate(pieces)])
        targets.append(pltpu.make_async_copy(done.at[c], out.at[of_whole], sems.at[3, c]))

    def work(c):
        values = embs[c].astype(jnp.float32)
        inverse = lax.rsqrt(jnp.sum(values * values, axis=-1, keepdims=True) + EPS)
        total = owns[c].astype(jnp.float32) + lasts[c].astype(jnp.float32)
        inner = jnp.sum(values * total, axis=-1, keepdims=True) * (inverse * inverse)
        done[c] = (inverse * (total - values * inner)).astype(jnp.bfloat16)

    chunked(chunks, sources, targets, work)


def finish(emb, own, last):
    rows, width = emb.shape
    chunks = 8
    held = pltpu.VMEM((chunks, rows // chunks, width), jnp.bfloat16)
    return pl.pallas_call(
        functools.partial(finish_kernel, chunks),
        in_specs=[ANY] * 5,
        out_specs=ANY,
        out_shape=jax.ShapeDtypeStruct(emb.shape, jnp.bfloat16),
        scratch_shapes=[held] * 4 + [pltpu.SemaphoreType.DMA((4, chunks))],
        **params(),
    )(emb, *own, *last)


def shift(value, axis, by):
    pairs_of = []
    for y in range(SIDE):
        for x in range(SIDE):
            to = (y * SIDE + (x + by) % SIDE) if axis == "x" else ((y + by) % SIDE * SIDE + x)
            pairs_of.append((y * SIDE + x, to))
    return lax.ppermute(value, "txt", pairs_of)


def after(values, done):
    out = lax.optimization_barrier(tuple(values) + tuple(done))
    return out[:len(values)]


def both_ways(axis, forward, backward, done=()):
    if done:
        (forward,), (backward,) = after((forward,), done[:1]), after((backward,), done[1:])
    return shift(forward, axis, 1), shift(backward, axis, -1)


def of_partner(value, axis, bit):
    return lax.ppermute(value, axis, [(i, i ^ bit) for i in range(lax.axis_size(axis))])


def join_kernel(chunks, ours_a, arrived_a, ours_b, arrived_b, out_a, out_b, ours, arrived, done, sems):
    step = 2 * ours_a.shape[0] // chunks
    sources, targets = [], []
    for c in range(chunks):
        mine, other, out = ((ours_a, arrived_a, out_a), (ours_b, arrived_b, out_b))[2 * c // chunks]
        rows = pl.ds(c * step % ours_a.shape[0], step)
        sources.append([
            pltpu.make_async_copy(mine.at[rows], ours.at[c], sems.at[0, c]),
            pltpu.make_async_copy(other.at[rows], arrived.at[c], sems.at[1, c])])
        targets.append(pltpu.make_async_copy(done.at[c], out.at[rows], sems.at[2, c]))

    def work(c):
        done[c] = (ours[c].astype(jnp.float32) + arrived[c].astype(jnp.float32)).astype(jnp.bfloat16)

    chunked(chunks, sources, targets, work)


def join(ours_a, arrived_a, ours_b, arrived_b):
    rows, width = ours_a.shape
    chunks = 4
    held = pltpu.VMEM((chunks, 2 * rows // chunks, width), jnp.bfloat16)
    return pl.pallas_call(
        functools.partial(join_kernel, chunks),
        in_specs=[ANY] * 4,
        out_specs=[ANY] * 2,
        out_shape=[jax.ShapeDtypeStruct(ours_a.shape, jnp.bfloat16)] * 2,
        scratch_shapes=[held] * 3 + [pltpu.SemaphoreType.DMA((3, chunks))],
        **params(),
    )(ours_a, arrived_a, ours_b, arrived_b)


def per_device(image_emb, text_emb, row_weight, log_scale, bias, pair_slots):
    width = image_emb.shape[1]
    half = HALF * ROWS
    scale = jnp.exp(log_scale[0])
    scalars = jnp.stack([scale, bias[0]])
    weights = jnp.pad(row_weight.reshape(BLK, ROWS), ((0, 0), (0, width - ROWS)))
    plan = jnp.pad(pair_slots.astype(jnp.bfloat16).reshape(1, -1), ((0, NOTES - BLK - 1), (0, width - SLOT_NUMBERS)))
    xa, xb, ya, yb = normalize(image_emb, text_emb, jnp.concatenate([weights, plan]))

    x1 = both_ways("x", xa, xb)
    y1 = both_ways("y", ya, yb)
    x2 = both_ways("x", *x1)
    y2 = both_ways("y", yb, ya, y1)
    x3 = both_ways("x", xb, xa, x2)
    y3 = both_ways("y", *y1, y2)
    y_next, y_prev = (y2[1], y1[1]), (y1[0], y2[0])
    own_x, own_y = (xa, xb), (ya, yb)

    notes = [message[half:half + BLK + 1, :ROWS].astype(jnp.float32) for message in (xa, x1[1], x2[0], x1[0])]
    weight_rows = jnp.concatenate([note[:BLK] for note in notes])
    plans = jnp.concatenate([note[BLK, :SLOT_NUMBERS] for note in notes]).astype(jnp.int32)
    me = lax.axis_index("txt")
    place = jnp.stack([me // SIDE, me % SIDE]).astype(jnp.int32)
    small = (plans, place, scalars, weight_rows)

    early_x = (*own_x, *own_x, *x2, *own_x)
    early_y = (*own_y, *y_next, *own_y, *y_prev)
    positives = tuple((POSITIVE, b) for b in range(BLK))
    early, early_stats, *dx_far = pairs(EARLY + positives, ("x",), (), small, early_x, early_y)
    early, early_stats, *arrived = lax.optimization_barrier((early, early_stats, *x3, *y3))
    x3, y3 = arrived[:2], arrived[2:]
    x_next, x_prev = (x3[1], x1[1]), (x1[0], x3[0])
    images = (*own_x, *x_next, *x2, *x_prev)
    texts = (*own_y, *y_next, *y3, *y_prev)

    opposite, opposite_stats, *far = pairs(OPPOSITE, ("x", "y"), tuple(dx_far), small, images, texts)
    x4 = both_ways("x", *far[:2])
    y4 = both_ways("y", *far[2:])
    late, late_stats = pairs(LATE, (), (), after(small, far), images, texts)
    coefs = (early, opposite, late)
    dx_next_a, dx_next_b, dx_prev_a, dx_prev_b = grads("x", (1, 3), False, small, texts, coefs)
    dy_next_a, dy_next_b, dy_prev_a, dy_prev_b = grads("y", (1, 3), False, small, images, coefs)

    sums = jnp.sum((early_stats + opposite_stats + late_stats).reshape(3, -1), axis=1)
    stats = jnp.stack([sums[0], sums[2], sums[1] / scale])
    stats = stats + of_partner(stats, "txt", 1)
    *x4, stats = lax.optimization_barrier((*x4, stats))
    x5 = both_ways("x", dx_next_b, dx_prev_a, x4)
    y5 = both_ways("y", dy_next_b, dy_prev_a, y4)
    joined_x = join(dx_next_a, x4[0], dx_prev_b, x4[1])
    joined_y = join(dy_next_a, y4[0], dy_prev_b, y4[1])
    for bit in (1, 2, 4):
        stats = stats + of_partner(stats, "img", bit)
    other = of_partner(stats, "txt", SIDE)
    *y5, other = lax.optimization_barrier((*y5, other))
    stats = stats + other
    x6 = both_ways("x", *joined_x, x5)
    y6 = both_ways("y", *joined_y, y5)
    own_small = after(small, (*x5, *y5))
    dx_own = grads("x", (0,), True, own_small, texts, coefs, (x5[1], x5[0]))
    dy_own = grads("y", (0,), True, own_small, images, coefs, (y5[1], y5[0]))
    stats = stats + of_partner(stats, "txt", 2 * SIDE)
    y6 = after(y6, (*dx_own, *dy_own))
    grad_text = finish(text_emb, dy_own, y6)
    *x6, stats = lax.optimization_barrier((*x6, stats, grad_text))[:3]
    wide = of_partner(jnp.broadcast_to(stats[:, None], (3, 1152)), "txt", 2)
    stats = stats + wide[:, 0]
    grad_image = finish(image_emb, dx_own, x6)
    count = BLK * ROWS * lax.axis_size("img") * lax.axis_size("txt")
    return (grad_image, grad_text, stats / count)


def solution(mesh):
    return jax.shard_map(
        per_device,
        mesh=mesh,
        in_specs=(
            P(("img", "txt"), None),
            P(("img", "txt"), None),
            P(("img", "txt")),
            P(),
            P(),
            P(("img", "txt"), None),
        ),
        out_specs=(P(("img", "txt"), None), P(("img", "txt"), None), P()),
        check_vma=False,
    )
```

```python
import functools

import jax
import jax.numpy as jnp
from jax import lax
from jax.experimental import pallas as pl
from jax.experimental.pallas import tpu as pltpu
from jax.sharding import PartitionSpec as P

ROWS = 384
BLK = 4
SIDE = 4
HALF = BLK // 2
EPS = 1e-06
VMEM = 60 * 1024 * 1024
CHUNK = 48

FAR = 2
EARLY = ((0, 1), (0, 3), (FAR, 0), (FAR, 1), (FAR, 3))
OPPOSITE = ((FAR, FAR), (0, FAR), (1, FAR), (3, FAR))
LATE = tuple((i, j) for i in (1, 3) for j in (0, 1, 3))
GROUPS = (EARLY, OPPOSITE, LATE)
COEF_AT = {slot: (source, known.index(slot)) for source, known in enumerate(GROUPS) for slot in known}
POSITIVE = "positive"
SLOT_NUMBERS = 3 * SIDE * SIDE
NOTES = 16
ANY = pl.BlockSpec(memory_space=pl.ANY)
SMEM = pl.BlockSpec(memory_space=pltpu.SMEM)
WHOLE = pl.BlockSpec(memory_space=pltpu.VMEM)


def params():
    return dict(
        compiler_params=pltpu.CompilerParams(vmem_limit_bytes=VMEM),
        cost_estimate=pl.CostEstimate(flops=1000, bytes_accessed=1000, transcendentals=0),
    )


def pipelined(items, ahead):
    for start, _, _ in items[:ahead]:
        start()
    for at, (_, wait, work) in enumerate(items):
        wait()
        if at + ahead < len(items):
            items[at + ahead][0]()
        work()


def chunked(chunks, sources, targets, work):
    def item(c):
        def start():
            for copy in sources[c]:
                copy.start()

        def wait():
            for copy in sources[c]:
                copy.wait()

        def run():
            work(c)
            targets[c].start()

        return start, wait, run

    pipelined([item(c) for c in range(chunks)], chunks)
    for copy in targets:
        copy.wait()


def normalize_kernel(chunks, images, texts, notes, xa, xb, ya, yb, held, done, sems, note_sems):
    half = images.shape[0] // 2
    step = 2 * half // chunks
    note_copies = [
        pltpu.make_async_copy(notes, out.at[pl.ds(half, NOTES)], note_sems.at[k]) for k, out in enumerate((xa, xb))]
    for copy in note_copies:
        copy.start()
    sources, targets = [], []
    for c in range(2 * chunks):
        emb, outs = ((images, (xa, xb)), (texts, (ya, yb)))[c // chunks]
        at = c % chunks * step
        sources.append([pltpu.make_async_copy(emb.at[pl.ds(at, step)], held.at[c], sems.at[0, c])])
        out = outs[at // half].at[pl.ds(at % half, step)]
        targets.append(pltpu.make_async_copy(done.at[c], out, sems.at[1, c]))

    def work(c):
        values = held[c].astype(jnp.float32)
        inverse = lax.rsqrt(jnp.sum(values * values, axis=-1, keepdims=True) + EPS)
        done[c] = (values * inverse).astype(jnp.bfloat16)

    chunked(2 * chunks, sources, targets, work)
    for copy in note_copies:
        copy.wait()


def normalize(images, texts, notes):
    rows, width = images.shape
    chunks = 4
    held = pltpu.VMEM((2 * chunks, rows // chunks, width), jnp.bfloat16)
    half = jax.ShapeDtypeStruct((rows // 2, width), jnp.bfloat16)
    noted = jax.ShapeDtypeStruct((rows // 2 + NOTES, width), jnp.bfloat16)
    return pl.pallas_call(
        functools.partial(normalize_kernel, chunks),
        in_specs=[ANY] * 3,
        out_specs=[ANY] * 4,
        out_shape=[noted, noted, half, half],
        scratch_shapes=[held, held, pltpu.SemaphoreType.DMA((2, 2 * chunks)), pltpu.SemaphoreType.DMA((2,))],
        **params(),
    )(images, texts, notes)


def when(condition, work):
    if condition is True:
        work()
    else:
        pl.when(condition)(work)


def block_copies(refs, offset, index, dst, sem):
    copies = []
    for part in range(2):
        if isinstance(index, int):
            local, inside = index % HALF, index // HALF == part
        else:
            local = jnp.clip(index - part * HALF, 0, HALF - 1)
            inside = (index >= part * HALF) & (index < (part + 1) * HALF)
        rows = pl.ds(local * ROWS if isinstance(index, int) else pl.multiple_of(local * ROWS, ROWS), ROWS)
        if inside is not False:
            copies.append((inside, pltpu.make_async_copy(refs[offset][part].at[rows], dst, sem)))
    return copies


def start_copies(live, copies):
    for inside, copy in copies:
        if inside is True or live is True:
            when(live if inside is True else inside, copy.start)
        else:
            when(live & inside, copy.start)


def split_refs(refs):
    return {offset: refs[2 * offset:2 * offset + 2] for offset in range(SIDE)}


N_REFS = 2 * SIDE


def columns(row):
    return jnp.transpose(jnp.broadcast_to(row, (128, ROWS)))


def coefficients(sims_ref, coef_ref, weight_ref, scale, offset, positive):
    def step(at, sums):
        loss_sum, coef_sum, dot_sum = sums
        rows = pl.ds(pl.multiple_of(at * CHUNK, CHUNK), CHUNK)
        sims = sims_ref[rows, :]
        logits = scale * sims + offset
        weight = jnp.concatenate([weight_ref[rows, :]] * (ROWS // 128), axis=1)
        scaled_weight = weight * scale
        if positive:
            row = lax.broadcasted_iota(jnp.int32, sims.shape, 0) + at * CHUNK
            col = lax.broadcasted_iota(jnp.int32, sims.shape, 1)
            diagonal = row == col
            logits = jnp.where(diagonal, -logits, logits)
            scaled_weight = jnp.where(diagonal, -scaled_weight, scaled_weight)
        power = jnp.exp(logits)
        one_more = 1.0 + power
        coef = scaled_weight * (power / one_more)
        loss = weight * jnp.log(one_more)
        coef_ref[rows, :] = coef.astype(jnp.bfloat16)

        def fold(value):
            return jnp.sum(value.reshape(CHUNK // 8, 8, ROWS), axis=0)

        return (loss_sum + fold(loss), coef_sum + fold(coef), dot_sum + fold(coef * sims))

    zero = jnp.zeros((8, ROWS), jnp.float32)
    return lax.fori_loop(0, ROWS // CHUNK, step, (zero, zero, zero), unroll=True)


def dot(lhs, rhs, dims):
    return lax.dot_general(lhs, rhs, (dims, ((), ())), preferred_element_type=jnp.float32)


NT = ((1,), (1,))
NN = ((1,), (0,))
TN = ((0,), (0,))


def read_entry(plans, place, slot):
    if slot[0] == POSITIVE:
        return slot[1], slot[1], True
    owner = (place[0] + slot[1]) % SIDE * SIDE + place[1]
    at = slot[0] * SLOT_NUMBERS + owner * 3
    return plans[at], plans[at + 1], plans[at + 2] > 0


def offsets_of(slot):
    return (0, 0) if slot[0] == POSITIVE else slot


def block_item(live, wanted, dst, sem, extra_copies, work):
    def start():
        for k, (refs, offset, index) in enumerate(wanted):
            start_copies(live, block_copies(refs, offset, index, dst[k], sem[k]))
        start_copies(live, [(True, copy) for copy in extra_copies])

    def wait():
        def waits():
            for k, (refs, offset, index) in enumerate(wanted):
                pltpu.make_async_copy(refs[0][0].at[pl.ds(0, ROWS)], dst[k], sem[k]).wait()
            for copy in extra_copies:
                copy.wait()

        when(live, waits)

    return start, wait, lambda: when(live, work)


def add_tile(acc, seen, index, tile):
    acc[index] = jnp.where(seen[index] > 0, acc[index], 0.0) + tile
    seen[index] = 1


def send_sums(acc, seen, staged, outs, sems, arrived=None):
    copies = []
    for b in range(BLK):
        total = jnp.where(seen[b] > 0, acc[b], 0.0)
        if arrived is not None:
            total = total + arrived[b].astype(jnp.float32)
        staged[b] = total.astype(staged.dtype)
        rows = pl.ds(b % HALF * ROWS, ROWS)
        copies.append(pltpu.make_async_copy(staged.at[b], outs[b // HALF].at[rows], sems.at[b]))
        copies[-1].start()
    return copies


def arrivals_of(parts, buf, sems):
    return [
        pltpu.make_async_copy(parts[b // HALF].at[pl.ds(b % HALF * ROWS, ROWS)], buf.at[b], sems.at[b])
        for b in range(BLK)]


def pairs_kernel(slots, sides, n_arrived, *refs):
    plans, place, scalars, image_rows = refs[0:4]
    at = 4
    xrefs, yrefs = split_refs(refs[at:at + N_REFS]), split_refs(refs[at + N_REFS:at + 2 * N_REFS])
    at += 2 * N_REFS
    arrived = refs[at:at + n_arrived]
    at += n_arrived
    coef_out, stats_out = refs[at], refs[at + 1]
    at += 2
    outs = refs[at:at + 2 * len(sides)]
    at += len(outs)
    xbuf, ybuf, wbuf, sims, coefs, sems, acc, seen, staged, osems = refs[at:at + 10]
    arrivals = arrivals_of(arrived, *refs[-2:]) if n_arrived else []
    scale, offset = scalars[0], scalars[1]
    copies = []

    def slot_item(s, slot):
        (i, j), (p, q, live) = offsets_of(slot), read_entry(plans, place, slot)

        def work():
            wbuf[...] = columns(image_rows[pl.ds(i * BLK + p, 1), :])
            for part in range(2):
                rows = pl.ds(part * (ROWS // 2), ROWS // 2)
                sims[rows, :] = dot(xbuf[s, rows, :], ybuf[s], NT)
            sums = coefficients(sims, coefs.at[s], wbuf, scale, offset, slot[0] == POSITIVE)
            for k in range(3):
                stats_out[k] += sums[k]
            pltpu.make_async_copy(coefs.at[s], coef_out.at[s], sems.at[2, s]).start()
            if "x" in sides and i == FAR:
                add_tile(acc.at[0], seen.at[0], p, dot(coefs[s], ybuf[s], NN))
            if "y" in sides and j == FAR:
                add_tile(acc.at[1], seen.at[1], q, dot(coefs[s], xbuf[s], TN))

        wanted = ((xrefs, i, p), (yrefs, j, q))
        return block_item(live, wanted, (xbuf.at[s], ybuf.at[s]), (sems.at[0, s], sems.at[1, s]), (), work)

    def send(side):
        for arrival in arrivals if side == 0 else ():
            arrival.wait()
        copies.extend(send_sums(
            acc.at[side], seen.at[side], staged.at[side], outs[2 * side:2 * side + 2], osems.at[side],
            refs[-2] if arrivals and side == 0 else None))

    stats_out[...] = jnp.zeros_like(stats_out)
    for side in range(len(sides)):
        for b in range(BLK):
            seen[side, b] = 0
    items = [slot_item(s, slot) for s, slot in enumerate(slots)]
    last = {"x": max([s for s, slot in enumerate(slots) if slot[0] == FAR], default=0), "y": len(slots) - 1}
    for side in reversed(range(len(sides))):
        at = last[sides[side]] + 1
        items.insert(at, (lambda: None, lambda: None, functools.partial(send, side)))
    items.insert(1, (lambda: [arrival.start() for arrival in arrivals], lambda: None, lambda: None))
    pipelined(items, 6)
    for s, slot in enumerate(slots):
        live = read_entry(plans, place, slot)[2]
        when(live, pltpu.make_async_copy(coefs.at[s], coef_out.at[s], sems.at[2, s]).wait)
    for copy in copies:
        copy.wait()


def pairs(slots, sides, arrived, small, images, texts):
    width = texts[0].shape[1]
    total = len(slots)
    held = max(len(sides), 1)
    blocks = (held, BLK, ROWS, width) if sides else (1, 1, 8, 128)
    out_shape = [
        jax.ShapeDtypeStruct((total, ROWS, ROWS), jnp.bfloat16),
        jax.ShapeDtypeStruct((3, 8, ROWS), jnp.float32),
    ] + [jax.ShapeDtypeStruct((HALF * ROWS, width), jnp.bfloat16)] * (2 * len(sides))
    scratch = [
        pltpu.VMEM((total, ROWS, width), jnp.bfloat16),
        pltpu.VMEM((total, ROWS, width), jnp.bfloat16),
        pltpu.VMEM((ROWS, 128), jnp.float32),
        pltpu.VMEM((ROWS, ROWS), jnp.float32),
        pltpu.VMEM((total, ROWS, ROWS), jnp.bfloat16),
        pltpu.SemaphoreType.DMA((3, total)),
        pltpu.VMEM(blocks, jnp.float32),
        pltpu.SMEM((held, BLK), jnp.int32),
        pltpu.VMEM(blocks, jnp.bfloat16),
        pltpu.SemaphoreType.DMA((held, BLK)),
    ]
    if arrived:
        scratch += [pltpu.VMEM((BLK, ROWS, width), jnp.bfloat16), pltpu.SemaphoreType.DMA((BLK,))]
    return pl.pallas_call(
        functools.partial(pairs_kernel, slots, sides, len(arrived)),
        in_specs=[SMEM, SMEM, SMEM, WHOLE] + [ANY] * (2 * N_REFS + len(arrived)),
        out_specs=[ANY, WHOLE] + [ANY] * (len(out_shape) - 2),
        out_shape=out_shape,
        scratch_shapes=scratch,
        **params(),
    )(*small, *images, *texts, *arrived)


def grads_kernel(axis, groups, n_arrived, *refs):
    plans, place = refs[0:2]
    other = split_refs(refs[2:2 + N_REFS])
    at = 2 + N_REFS
    coefs = refs[at:at + len(GROUPS)]
    arrived = refs[at + len(GROUPS):at + len(GROUPS) + n_arrived]
    at += len(GROUPS) + n_arrived
    outs = refs[at:at + 2 * len(groups)]
    buf, cbuf, acc, seen, staged, sems, osems = refs[at + 2 * len(groups):at + 2 * len(groups) + 7]
    mine = 0 if axis == "x" else 1
    dims = NN if axis == "x" else TN
    items, copies, arrivals = [], [], []
    if n_arrived:
        abuf, asems = refs[-2:]
        arrivals = arrivals_of(arrived, abuf, asems)

    def slot_item(at, group, last, slot, source, index):
        entry = read_entry(plans, place, slot)
        copy = pltpu.make_async_copy(coefs[source].at[index], cbuf.at[at], sems.at[1, at])

        def work():
            add_tile(acc.at[group], seen.at[group], entry[mine], dot(cbuf[at], buf[at], dims))

        wanted = ((other, offsets_of(slot)[1 - mine], entry[1 - mine]),)
        start, wait, run = block_item(entry[2], wanted, (buf.at[at],), (sems.at[0, at],), (copy,), work)

        def run_and_send():
            run()
            if last:
                for arrival in arrivals:
                    arrival.wait()
                copies.extend(send_sums(
                    acc.at[group], seen.at[group], staged.at[group], outs[2 * group:2 * group + 2], osems.at[group],
                    abuf if n_arrived else None))

        return start, wait, run_and_send

    for group, entries in enumerate(groups):
        for b in range(BLK):
            seen[group, b] = 0
        for entry in entries:
            items.append(slot_item(len(items), group, entry is entries[-1], *entry))
    for arrival in arrivals:
        arrival.start()
    pipelined(items, 5)
    for copy in copies:
        copy.wait()


def grads(axis, offsets, with_positive, small, blocks, coefs, arrived=()):
    width = blocks[0].shape[1]
    groups = []
    for offset in offsets:
        group = []
        for neighbour in (0, 1, 3, 2):
            slot = (offset, neighbour) if axis == "x" else (neighbour, offset)
            if slot != (0, 0):
                group.append((slot, *COEF_AT[slot]))
        if with_positive:
            group += [((POSITIVE, b), 0, len(EARLY) + b) for b in range(BLK)]
        groups.append(tuple(group))
    total = sum(len(group) for group in groups)
    scratch = [
        pltpu.VMEM((total, ROWS, width), jnp.bfloat16),
        pltpu.VMEM((total, ROWS, ROWS), jnp.bfloat16),
        pltpu.VMEM((len(groups), BLK, ROWS, width), jnp.float32),
        pltpu.SMEM((len(groups), BLK), jnp.int32),
        pltpu.VMEM((len(groups), BLK, ROWS, width), jnp.bfloat16),
        pltpu.SemaphoreType.DMA((2, total)),
        pltpu.SemaphoreType.DMA((len(groups), BLK)),
    ]
    if arrived:
        scratch += [pltpu.VMEM((BLK, ROWS, width), jnp.bfloat16), pltpu.SemaphoreType.DMA((BLK,))]
    return pl.pallas_call(
        functools.partial(grads_kernel, axis, tuple(groups), len(arrived)),
        in_specs=[SMEM, SMEM] + [ANY] * (N_REFS + len(GROUPS) + len(arrived)),
        out_specs=[ANY] * (2 * len(groups)),
        out_shape=[jax.ShapeDtypeStruct((HALF * ROWS, width), jnp.bfloat16)] * (2 * len(groups)),
        scratch_shapes=scratch,
        **params(),
    )(*small[:2], *blocks, *coefs, *arrived)


def finish_kernel(chunks, emb, own_a, own_b, last_a, last_b, out, embs, owns, lasts, done, sems):
    half = own_a.shape[0]
    step = 2 * half // chunks
    sources, targets = [], []
    for c in range(chunks):
        own, last = ((own_a, last_a), (own_b, last_b))[c * step // half]
        rows, of_whole = pl.ds(c * step % half, step), pl.ds(c * step, step)
        pieces = ((emb, of_whole, embs), (own, rows, owns), (last, rows, lasts))
        sources.append([
            pltpu.make_async_copy(ref.at[at], held.at[c], sems.at[k, c]) for k, (ref, at, held) in enumerate(pieces)])
        targets.append(pltpu.make_async_copy(done.at[c], out.at[of_whole], sems.at[3, c]))

    def work(c):
        values = embs[c].astype(jnp.float32)
        inverse = lax.rsqrt(jnp.sum(values * values, axis=-1, keepdims=True) + EPS)
        total = owns[c].astype(jnp.float32) + lasts[c].astype(jnp.float32)
        inner = jnp.sum(values * total, axis=-1, keepdims=True) * (inverse * inverse)
        done[c] = (inverse * (total - values * inner)).astype(jnp.bfloat16)

    chunked(chunks, sources, targets, work)


def finish(emb, own, last):
    rows, width = emb.shape
    chunks = 8
    held = pltpu.VMEM((chunks, rows // chunks, width), jnp.bfloat16)
    return pl.pallas_call(
        functools.partial(finish_kernel, chunks),
        in_specs=[ANY] * 5,
        out_specs=ANY,
        out_shape=jax.ShapeDtypeStruct(emb.shape, jnp.bfloat16),
        scratch_shapes=[held] * 4 + [pltpu.SemaphoreType.DMA((4, chunks))],
        **params(),
    )(emb, *own, *last)


def shift(value, axis, by):
    pairs_of = []
    for y in range(SIDE):
        for x in range(SIDE):
            to = (y * SIDE + (x + by) % SIDE) if axis == "x" else ((y + by) % SIDE * SIDE + x)
            pairs_of.append((y * SIDE + x, to))
    return lax.ppermute(value, "txt", pairs_of)


def after(values, done):
    out = lax.optimization_barrier(tuple(values) + tuple(done))
    return out[:len(values)]


def both_ways(axis, forward, backward, done=()):
    if done:
        (forward,), (backward,) = after((forward,), done[:1]), after((backward,), done[1:])
    return shift(forward, axis, 1), shift(backward, axis, -1)


def of_partner(value, axis, bit):
    return lax.ppermute(value, axis, [(i, i ^ bit) for i in range(lax.axis_size(axis))])


def join_kernel(chunks, ours_a, arrived_a, ours_b, arrived_b, out_a, out_b, ours, arrived, done, sems):
    step = 2 * ours_a.shape[0] // chunks
    sources, targets = [], []
    for c in range(chunks):
        mine, other, out = ((ours_a, arrived_a, out_a), (ours_b, arrived_b, out_b))[2 * c // chunks]
        rows = pl.ds(c * step % ours_a.shape[0], step)
        sources.append([
            pltpu.make_async_copy(mine.at[rows], ours.at[c], sems.at[0, c]),
            pltpu.make_async_copy(other.at[rows], arrived.at[c], sems.at[1, c])])
        targets.append(pltpu.make_async_copy(done.at[c], out.at[rows], sems.at[2, c]))

    def work(c):
        done[c] = (ours[c].astype(jnp.float32) + arrived[c].astype(jnp.float32)).astype(jnp.bfloat16)

    chunked(chunks, sources, targets, work)


def join(ours_a, arrived_a, ours_b, arrived_b):
    rows, width = ours_a.shape
    chunks = 4
    held = pltpu.VMEM((chunks, 2 * rows // chunks, width), jnp.bfloat16)
    return pl.pallas_call(
        functools.partial(join_kernel, chunks),
        in_specs=[ANY] * 4,
        out_specs=[ANY] * 2,
        out_shape=[jax.ShapeDtypeStruct(ours_a.shape, jnp.bfloat16)] * 2,
        scratch_shapes=[held] * 3 + [pltpu.SemaphoreType.DMA((3, chunks))],
        **params(),
    )(ours_a, arrived_a, ours_b, arrived_b)


def per_device(image_emb, text_emb, row_weight, log_scale, bias, pair_slots):
    width = image_emb.shape[1]
    half = HALF * ROWS
    scale = jnp.exp(log_scale[0])
    scalars = jnp.stack([scale, bias[0]])
    weights = jnp.pad(row_weight.reshape(BLK, ROWS), ((0, 0), (0, width - ROWS)))
    plan = jnp.pad(pair_slots.reshape(1, -1), ((0, NOTES - BLK - 1), (0, width - SLOT_NUMBERS))).astype(jnp.bfloat16)
    xa, xb, ya, yb = normalize(image_emb, text_emb, jnp.concatenate([weights, plan]))

    x1 = both_ways("x", xa, xb)
    y1 = both_ways("y", ya, yb)
    x2 = both_ways("x", *x1)
    y2 = both_ways("y", yb, ya, y1)
    x3 = both_ways("x", xb, xa, x2)
    y3 = both_ways("y", *y1, y2)
    y_next, y_prev = (y2[1], y1[1]), (y1[0], y2[0])
    own_x, own_y = (xa, xb), (ya, yb)

    notes = [message[half:half + BLK + 1, :ROWS].astype(jnp.float32) for message in (xa, x1[1], x2[0], x1[0])]
    weight_rows = jnp.concatenate([note[:BLK] for note in notes])
    plans = jnp.concatenate([note[BLK, :SLOT_NUMBERS] for note in notes]).astype(jnp.int32)
    me = lax.axis_index("txt")
    place = jnp.stack([me // SIDE, me % SIDE]).astype(jnp.int32)
    small = (plans, place, scalars, weight_rows)

    early_x = (*own_x, *own_x, *x2, *own_x)
    early_y = (*own_y, *y_next, *own_y, *y_prev)
    positives = tuple((POSITIVE, b) for b in range(BLK))
    early, early_stats, *dx_far = pairs(EARLY + positives, ("x",), (), small, early_x, early_y)
    early, early_stats, *arrived = lax.optimization_barrier((early, early_stats, *x3, *y3))
    x3, y3 = arrived[:2], arrived[2:]
    x_next, x_prev = (x3[1], x1[1]), (x1[0], x3[0])
    images = (*own_x, *x_next, *x2, *x_prev)
    texts = (*own_y, *y_next, *y3, *y_prev)

    opposite, opposite_stats, *far = pairs(OPPOSITE, ("x", "y"), tuple(dx_far), small, images, texts)
    x4 = both_ways("x", *far[:2])
    y4 = both_ways("y", *far[2:])
    late, late_stats = pairs(LATE, (), (), after(small, far), images, texts)
    coefs = (early, opposite, late)
    dx_next_a, dx_next_b, dx_prev_a, dx_prev_b = grads("x", (1, 3), False, small, texts, coefs)
    dy_next_a, dy_next_b, dy_prev_a, dy_prev_b = grads("y", (1, 3), False, small, images, coefs)

    sums = jnp.sum((early_stats + opposite_stats + late_stats).reshape(3, -1), axis=1)
    stats = jnp.stack([sums[0], sums[2], sums[1] / scale])
    stats = stats + of_partner(stats, "txt", 1)
    *x4, stats = lax.optimization_barrier((*x4, stats))
    x5 = both_ways("x", dx_next_b, dx_prev_a, x4)
    y5 = both_ways("y", dy_next_b, dy_prev_a, y4)
    joined_x = join(dx_next_a, x4[0], dx_prev_b, x4[1])
    joined_y = join(dy_next_a, y4[0], dy_prev_b, y4[1])
    for bit in (1, 2, 4):
        stats = stats + of_partner(stats, "img", bit)
    other = of_partner(stats, "txt", SIDE)
    *y5, other = lax.optimization_barrier((*y5, other))
    stats = stats + other
    x6 = both_ways("x", *joined_x, x5)
    y6 = both_ways("y", *joined_y, y5)
    own_small = after(small, (*x5, *y5))
    dx_own = grads("x", (0,), True, own_small, texts, coefs, (x5[1], x5[0]))
    dy_own = grads("y", (0,), True, own_small, images, coefs, (y5[1], y5[0]))
    stats = stats + of_partner(stats, "txt", 2 * SIDE)
    y6 = after(y6, (*dx_own, *dy_own))
    grad_text = finish(text_emb, dy_own, y6)
    *x6, stats = lax.optimization_barrier((*x6, stats, grad_text))[:3]
    wide = of_partner(jnp.broadcast_to(stats[:, None], (3, 1152)), "txt", 2)
    stats = stats + wide[:, 0]
    grad_image = finish(image_emb, dx_own, x6)
    count = BLK * ROWS * lax.axis_size("img") * lax.axis_size("txt")
    return (grad_image, grad_text, stats / count)


def solution(mesh):
    return jax.shard_map(
        per_device,
        mesh=mesh,
        in_specs=(
            P(("img", "txt"), None),
            P(("img", "txt"), None),
            P(("img", "txt")),
            P(),
            P(),
            P(("img", "txt"), None),
        ),
        out_specs=(P(("img", "txt"), None), P(("img", "txt"), None), P()),
        check_vma=False,
    )
```
